512 devices in a mesh: group: 64 (over x, y, z_hi, core), tp: 8 (over z_lo).
Axes of the slice: x: 4, y: 4, z: 16 (z_hi: 2, z_lo: 8; z = z_hi * 8 + z_lo), core: 2. Of those that a mesh axis runs over, the one named last changes fastest.
Arguments:
- hidden: bfloat16 [4, 256, 5120], P(None, 'group', 'tp'), may hold values from -6 to 6
- queries: bfloat16 [4, 256, 8192], P(None, 'group', 'tp'), may hold values from -300 to 300
- stored_key_cache: bfloat16 [256, 1024, 1024], P('group', None, 'tp'), may hold values from -6 to 6
- stored_value_cache: bfloat16 [256, 1024, 1024], P('group', None, 'tp'), may hold values from -6 to 6
- lengths: int32 [256], P('group'), may hold values from 2 to 1024, as said below
- base_key_value_weight: bfloat16 [5120, 2048], P(None, 'tp'), may hold values from -0.078125 to 0.078125
- adapter_down_weight: bfloat16 [64, 5120], P('group', 'tp'), may hold values from -0.078125 to 0.078125
- adapter_up_weight: bfloat16 [64, 2048], P('group', 'tp'), may hold values from -0.75 to 0.75
- key_norm_gain: float32 [128], replicated, may hold values from 0.1 to 1.9
Outputs:
- attention: bfloat16 [4, 256, 8192], P(None, 'group', 'tp')
- new_entries: bfloat16 [4, 256, 2048], P(None, 'group', 'tp')
The draws below stay inside these ranges and needn't reach their ends.
Inputs may be any that keep to these rules, and one draw needn't show every extreme that they name: `lengths`: in every block of 4 rows of one rollout group some row has exactly 1024 filled slots.
All inputs are finite; a program needn't handle non-finite values.
Results may differ from the reference program's by a relative error of at most 0.0055.
Values may be sent and summed in bfloat16 or wider, within the bound.
A program may use at most 64 MiB of HBM per device.

```python
import jax
import jax.numpy as jnp
from jax import lax

MODEL_WIDTH = 5120
QH = 64
KVH = 8
HEAD = 128
ADAPTER_RANK = 64
STEPS = 4
ROWS = 4
CTX = 1024
ROWS_ALL = 256
KEY_VALUE_WIDTH = 2048


def cache_block(key):
    return jnp.clip(jax.random.normal(key, (ROWS_ALL, CTX, KVH * HEAD), jnp.float32), -6.0, 6.0)


def draw_stored_key_cache(key, part):
    return cache_block(key).astype(jnp.bfloat16)


def draw_queries(key, part):
    key = jax.random.fold_in(key, 5)
    values = jnp.clip(jax.random.normal(key, (STEPS, ROWS_ALL, QH * HEAD), jnp.float32), -6.0, 6.0)
    return jnp.clip(values, -300.0, 300.0).astype(jnp.bfloat16)


def draw_lengths(key, part):
    key = jax.random.fold_in(key, 3)
    drawn = jax.random.randint(key, (ROWS_ALL,), 2, CTX + 1)
    blocks = ROWS_ALL // ROWS
    picked = jax.random.randint(jax.random.fold_in(key, 1), (blocks, 1), 0, ROWS)
    filled = (jnp.arange(ROWS, dtype=jnp.int32)[None, :] == picked).reshape(ROWS_ALL)
    return jnp.where(filled, CTX, drawn).astype(jnp.int32)


def block_levels(own_key, extent, split, least, top_value):
    gain = 1.0
    for axis_at, parts in split:
        heights = jax.random.uniform(jax.random.fold_in(jax.random.fold_in(own_key, 6), axis_at), (parts,), jnp.float32, least / len(split), top_value / len(split))
        gain = gain * jnp.repeat(jnp.exp(heights), extent[axis_at] // parts).reshape((-1,) + (1,) * (len(extent) - 1 - axis_at))
    return gain


def noise(rng, dims, scale, bound, shards=(), kind=jnp.bfloat16):
    entries = scale * jax.random.normal(rng, dims, jnp.float32)
    if shards:
        entries = entries * block_levels(rng, dims, shards, -0.22, 0.18)
    return jnp.clip(entries, -bound, bound).astype(kind)


def setup_inputs(seed: int = 0) -> dict:
    seeds = jax.random.split(jax.random.key(seed), 10)
    return {
        "hidden": noise(seeds[0], (STEPS, ROWS_ALL, MODEL_WIDTH), 1.0, 6.0, ((1, 64), (2, 8))),
        "queries": draw_queries(jax.random.fold_in(seeds[9], 71), 0),
        "stored_key_cache": draw_stored_key_cache(jax.random.fold_in(seeds[9], 71), 0),
        "stored_value_cache": noise(seeds[3], (ROWS_ALL, CTX, KVH * HEAD), 1.0, 6.0, ((0, 64), (2, 8))),
        "lengths": draw_lengths(jax.random.fold_in(seeds[9], 71), 0),
        "base_key_value_weight": noise(seeds[5], (MODEL_WIDTH, KEY_VALUE_WIDTH), MODEL_WIDTH ** -0.5, 0.078125, ((1, 8),)),
        "adapter_down_weight": noise(seeds[6], (ADAPTER_RANK, MODEL_WIDTH), MODEL_WIDTH ** -0.5, 0.078125, ((0, 64), (1, 8))),
        "adapter_up_weight": noise(seeds[7], (ADAPTER_RANK, KEY_VALUE_WIDTH), ADAPTER_RANK ** -0.5, 0.75, ((0, 64), (1, 8))),
        "key_norm_gain": jnp.clip(1.0 + 0.18 * jax.random.normal(seeds[8], (HEAD,), jnp.float32), 0.1, 1.9),
    }


adapter_scale = 2.0
norm_eps = 1e-06

def attend_row(operands):
    query_row, key_row, value_row, length, fresh_keys, fresh_values = operands
    groups = QH // KVH
    query_row = query_row.astype(jnp.float32).reshape(STEPS, KVH, groups, HEAD)
    key_row = key_row.astype(jnp.float32).reshape(CTX, KVH, HEAD)
    value_row = value_row.astype(jnp.float32).reshape(CTX, KVH, HEAD)
    fresh_keys = fresh_keys.astype(jnp.float32)
    fresh_values = fresh_values.astype(jnp.float32)
    factor = HEAD ** (-0.5)
    cached = jnp.einsum('sjgh,cjh->sjgc', query_row, key_row) * factor
    valid = jnp.arange(CTX, dtype=jnp.int32) < length
    cached = jnp.where(valid[None, None, None, :], cached, -jnp.inf)
    recent = jnp.einsum('sjgh,tjh->sjgt', query_row, fresh_keys) * factor
    causal = jnp.arange(STEPS, dtype=jnp.int32)[None, :] <= jnp.arange(STEPS, dtype=jnp.int32)[:, None]
    recent = jnp.where(causal[:, None, None, :], recent, -jnp.inf)
    top = jnp.maximum(lax.optimization_barrier(jnp.max(cached, axis=-1, keepdims=True)), lax.optimization_barrier(jnp.max(recent, axis=-1, keepdims=True)))
    cached_exp = jnp.exp(cached - top)
    recent_exp = jnp.exp(recent - top)
    total = lax.optimization_barrier(jnp.sum(cached_exp, axis=-1, keepdims=True)) + lax.optimization_barrier(jnp.sum(recent_exp, axis=-1, keepdims=True))
    cached_w = (cached_exp / total).astype(jnp.bfloat16).astype(jnp.float32)
    recent_w = (recent_exp / total).astype(jnp.bfloat16).astype(jnp.float32)
    result = jnp.einsum('sjgc,cjh->sjgh', cached_w, value_row) + jnp.einsum('sjgt,tjh->sjgh', recent_w, fresh_values)
    return result.reshape(STEPS, QH * HEAD).astype(jnp.bfloat16)

def reference(hidden, queries, stored_key_cache, stored_value_cache, lengths, base_key_value_weight, adapter_down_weight, adapter_up_weight, key_norm_gain):
    adapter_update = lax.dot_general(adapter_down_weight, adapter_up_weight, (((0,), (0,)), ((), ())), preferred_element_type=jnp.float32)
    merged_weight = base_key_value_weight.astype(jnp.float32) + adapter_scale * adapter_update
    flat = hidden.astype(jnp.float32).reshape(STEPS * ROWS_ALL, MODEL_WIDTH)
    projected = jnp.dot(flat, merged_weight, precision=lax.Precision.HIGHEST).reshape(STEPS, ROWS_ALL, KVH, 2, HEAD)
    raw_keys = projected[:, :, :, 0, :]
    values = projected[:, :, :, 1, :]
    scale = lax.rsqrt(lax.optimization_barrier(jnp.mean(raw_keys * raw_keys, axis=-1, keepdims=True)) + norm_eps)
    new_keys = (raw_keys * scale * key_norm_gain.astype(jnp.float32)).astype(jnp.bfloat16)
    new_values = values.astype(jnp.bfloat16)
    new_entries = jnp.stack([new_keys, new_values], axis=3).reshape(STEPS, ROWS_ALL, KEY_VALUE_WIDTH)
    per_row = lax.map(attend_row, (jnp.transpose(queries, (1, 0, 2)), stored_key_cache, stored_value_cache, lengths, jnp.transpose(new_keys, (1, 0, 2, 3)), jnp.transpose(new_values, (1, 0, 2, 3))))
    attention = jnp.transpose(per_row, (1, 0, 2))
    return (attention, new_entries)
```

```python
import functools

import jax
import jax.numpy as jnp
from jax import lax
from jax.experimental import pallas as pl
from jax.experimental.pallas import tpu as pltpu
from jax.sharding import PartitionSpec as P

HEAD = 128
STEPS = 4
ROWS = 4
HEADS = 8
TOKENS = STEPS * ROWS
QUERIES = STEPS * HEADS
TP = 8
PLANE = 32
KB = 5
UP = 3

ADAPTER_SCALE = 2.0
NORM_EPS = 1e-06
MESH = pl.DeviceIdType.MESH
BF = jnp.bfloat16
F32 = jnp.float32


def dot(a, b):
    return jnp.dot(a, b, preferred_element_type=F32)


def dot_t(a, b):
    return lax.dot_general(a, b, (((1,), (1,)), ((), ())), preferred_element_type=F32)


def kernel(
    hidden_hbm, queries_hbm, keys_hbm, values_hbm, lengths_hbm, weight_hbm, down_hbm, up_hbm, gain_hbm,
    att_ref, ent_ref,
    hidden_v, queries_v, keys_v, values_v, lengths_s, weight_v, down_v, up_v, gain_v,
    hf, q32, o32, tiles, hall, relay_up, relay_down, partner, bbuf, usend, urecv,
    loc_sem, kv_sem, tile_sem, hall_sem, relay_sem, partner_sem, b_sem, u_sem,
):
    g = lax.axis_index("group")
    t = lax.axis_index("tp")
    xy, zh, c = g // 4, (g // 2) % 2, g % 2
    z = zh * 8 + t
    me = xy * 2 + c

    def at_z(where):
        where = where % 16
        return (xy * 4 + (where // 8) * 2 + c, where % 8)

    def in_plane(i):
        p = (me + 1 + i) % PLANE
        return ((p // 2) * 4 + zh * 2 + p % 2, t)

    def remote(src, dst, send, recv, to):
        return pltpu.make_async_remote_copy(
            src_ref=src, dst_ref=dst, send_sem=send, recv_sem=recv, device_id=to, device_id_type=MESH
        )

    def wait_bytes(ref, sem):
        pltpu.make_async_copy(ref, ref, sem).wait()

    small = [
        pltpu.make_async_copy(src, dst, loc_sem.at[i])
        for i, (src, dst) in enumerate(
            (
                (hidden_hbm, hidden_v),
                (down_hbm, down_v),
                (up_hbm, up_v),
                (queries_hbm, queries_v),
                (lengths_hbm, lengths_s),
                (gain_hbm, gain_v),
                (weight_hbm, weight_v),
            )
        )
    ]
    for copy in small[:6]:
        copy.start()
    barrier = pltpu.get_barrier_semaphore()

    def greet_plane(i, _):
        pl.semaphore_signal(barrier, inc=1, device_id=in_plane(i), device_id_type=MESH)
        return 0

    lax.fori_loop(0, PLANE - 1, greet_plane, 0)

    def greet_z(i, _):
        pl.semaphore_signal(barrier, inc=1, device_id=at_z(z + 1 + i), device_id_type=MESH)
        pl.semaphore_signal(barrier, inc=1, device_id=at_z(z + 15 - i), device_id_type=MESH)
        return 0

    lax.fori_loop(0, 4, greet_z, 0)

    kv = []
    for r in range(ROWS):
        kv.append(
            (
                pltpu.make_async_copy(keys_hbm.at[r], keys_v.at[r], kv_sem.at[0, r]),
                pltpu.make_async_copy(values_hbm.at[r], values_v.at[r], kv_sem.at[1, r]),
            )
        )
        kv[r][0].start()
        kv[r][1].start()
    small[6].start()

    small[0].wait()
    for s in range(STEPS):
        hf[s * ROWS : (s + 1) * ROWS, :] = hidden_v[s].astype(F32)
    for k in range(KB):
        hall[t, k] = hf[:, k * HEAD : (k + 1) * HEAD].astype(BF)
    small[1].wait()
    small[2].wait()
    down = down_v[...].astype(F32)
    up = up_v[...].astype(F32)
    for k in range(KB):
        tiles[me, k : k + 1, :] = down[:, k * HEAD : (k + 1) * HEAD]
    for k in range(2):
        tiles[me, KB + k : KB + k + 1, :] = up[:, k * HEAD : (k + 1) * HEAD]
    tiles[me, 7:8, :] = jnp.zeros((1, HEAD), F32)

    pl.semaphore_wait(barrier, PLANE - 1 + 8)

    first_up = remote(hall.at[t, pl.ds(0, UP)], relay_up, relay_sem.at[0, 0], relay_sem.at[0, 1], at_z(z + 4))
    first_down = remote(
        hall.at[t, pl.ds(UP, KB - UP)], relay_down, relay_sem.at[1, 0], relay_sem.at[1, 1], at_z(z + 12)
    )
    first_up.start()
    first_down.start()

    def send_tile(i, _):
        remote(tiles.at[me], tiles.at[me], tile_sem.at[0], tile_sem.at[1], in_plane(i)).start()
        return 0

    lax.fori_loop(0, PLANE - 1, send_tile, 0)

    def send_hidden(d):
        @pl.when(t + d < TP)
        def _():
            remote(hall.at[t], hall.at[t], hall_sem.at[0], hall_sem.at[1], (g, t + d)).start()

        @pl.when(t >= d)
        def _():
            remote(hall.at[t], hall.at[t], hall_sem.at[0], hall_sem.at[1], (g, t - d)).start()

    for d in range(1, 5):
        send_hidden(d)

    small[3].wait()
    for s in range(STEPS):
        for h in range(HEADS):
            q32[pl.ds(s * HEADS + h, ROWS, stride=QUERIES), :] = queries_v[
                s, :, h * HEAD : (h + 1) * HEAD
            ].astype(F32)
    small[4].wait()
    factor = HEAD ** (-0.5)

    def cached(r):
        kv[r][0].wait()
        q = q32[r * QUERIES : (r + 1) * QUERIES, :].astype(BF)
        scores = dot_t(q, keys_v[r]) * factor
        slot = lax.broadcasted_iota(jnp.int32, scores.shape, 1)
        scores = jnp.where(slot < lengths_s[r], scores, -jnp.inf)
        top = jnp.max(scores, axis=1, keepdims=True)
        p = jnp.exp(scores - top)
        total = jnp.sum(p, axis=1, keepdims=True)
        kv[r][1].wait()
        return top, total, dot(p.astype(BF), values_v[r])

    rows = [cached(0), cached(1)]

    first_up.wait_recv()
    second_up = remote(relay_up, partner.at[pl.ds(0, UP)], partner_sem.at[0, 0], partner_sem.at[0, 1], at_z(z + 4))
    second_up.start()
    first_down.wait_recv()
    second_down = remote(
        relay_down, partner.at[pl.ds(UP, KB - UP)], partner_sem.at[1, 0], partner_sem.at[1, 1], at_z(z + 12)
    )
    second_down.start()
    for d in range(5, 8):
        send_hidden(d)

    rows += [cached(2), cached(3)]

    wait_bytes(tiles.at[pl.ds(0, PLANE - 1)], tile_sem.at[1])
    a = []
    for k in range(KB):
        block = tiles_rows(tiles, k)
        a.append(jnp.concatenate([block] * 4, axis=0))
    a = jnp.concatenate(a, axis=1)
    bbuf[0, :, 0:HEAD] = tiles_rows(tiles, KB)
    bbuf[0, :, HEAD : 2 * HEAD] = tiles_rows(tiles, KB + 1)
    send_b = remote(bbuf.at[0], bbuf.at[1], b_sem.at[0], b_sem.at[1], at_z(z + 8))
    send_b.start()

    def parts(blocks):
        u = dot_t(jnp.concatenate(blocks, axis=1), a)
        high = u.astype(BF).astype(F32)
        rest = u - high
        mid = rest.astype(BF).astype(F32)
        low = (rest - mid).astype(BF).astype(F32)
        lane = lax.broadcasted_iota(jnp.int32, u.shape, 1)
        zero = jnp.zeros_like(u)
        packed = jnp.where(lane < 32, high, jnp.where(lane < 64, mid, jnp.where(lane < 96, low, zero)))
        return packed.astype(BF)

    urecv[0, t] = parts([hall[t, k] for k in range(KB)])

    def send_own(i, _):
        remote(urecv.at[0, t], urecv.at[0, t], u_sem.at[0, 0], u_sem.at[0, 1], (g, (t + 1 + i) % TP)).start()
        return 0

    lax.fori_loop(0, TP - 1, send_own, 0)

    second_up.wait_recv()
    second_down.wait_recv()
    usend[...] = parts([partner[k] for k in range(KB)])
    other = xy * 4 + (1 - zh) * 2 + c

    def send_cross(i, _):
        remote(usend, urecv.at[1, t], u_sem.at[1, 0], u_sem.at[1, 1], (other, (t + i) % TP)).start()
        return 0

    lax.fori_loop(0, TP, send_cross, 0)

    wait_bytes(hall.at[pl.ds(0, TP - 1)], hall_sem.at[1])
    small[6].wait()
    base = jnp.zeros((TOKENS, 2 * HEAD), F32)
    for i in range(TP):
        block = jnp.concatenate([hall[i, k] for k in range(KB)], axis=1)
        base = base + dot(block, weight_v[i * KB * HEAD : (i + 1) * KB * HEAD, :])

    top_c = jnp.concatenate([r[0] for r in rows], axis=0)
    total_c = jnp.concatenate([r[1] for r in rows], axis=0)
    acc_c = jnp.concatenate([r[2] for r in rows], axis=0)
    small[5].wait()
    gain = gain_v[...].reshape(1, HEAD)

    send_b.wait_recv()
    b_own = jnp.concatenate([bbuf[0]] * 4, axis=0)
    b_other = jnp.concatenate([bbuf[1]] * 4, axis=0)
    wait_bytes(urecv.at[0, pl.ds(0, TP - 1)], u_sem.at[0, 1])
    update = dot(urecv[0].reshape(TP * TOKENS, HEAD), b_own)
    wait_bytes(urecv.at[1], u_sem.at[1, 1])
    update = update + dot(urecv[1].reshape(TP * TOKENS, HEAD), b_other)
    update = jnp.sum(update.reshape(TP, TOKENS, 2 * HEAD), axis=0)
    projected = base + ADAPTER_SCALE * update

    raw = projected[:, 0:HEAD]
    value = projected[:, HEAD : 2 * HEAD]
    scale = lax.rsqrt(jnp.mean(raw * raw, axis=1, keepdims=True) + NORM_EPS)
    key = raw * scale * gain
    for s in range(STEPS):
        ent_ref[s, :, 0:HEAD] = key[s * ROWS : (s + 1) * ROWS].astype(BF)
        ent_ref[s, :, HEAD : 2 * HEAD] = value[s * ROWS : (s + 1) * ROWS].astype(BF)

    scores = dot_t(q32[...].astype(BF), key.astype(BF)) * factor
    qi = lax.broadcasted_iota(jnp.int32, scores.shape, 0)
    ki = lax.broadcasted_iota(jnp.int32, scores.shape, 1)
    seen = (ki % ROWS == qi // QUERIES) & (ki // ROWS <= (qi % QUERIES) // HEADS)
    scores = jnp.where(seen, scores, -jnp.inf)
    top = jnp.maximum(top_c, jnp.max(scores, axis=1, keepdims=True))
    p = jnp.exp(scores - top)
    carry = jnp.exp(top_c - top)
    total = carry * total_c + jnp.sum(p, axis=1, keepdims=True)
    result = (carry * acc_c + dot(p.astype(BF), value.astype(BF))) / total
    o32[...] = result
    for s in range(STEPS):
        for h in range(HEADS):
            att_ref[s, :, h * HEAD : (h + 1) * HEAD] = o32[
                pl.ds(s * HEADS + h, ROWS, stride=QUERIES), :
            ].astype(BF)

    first_up.wait_send()
    first_down.wait_send()
    second_up.wait_send()
    second_down.wait_send()
    send_b.wait_send()
    wait_bytes(tiles.at[pl.ds(0, PLANE - 1)], tile_sem.at[0])
    wait_bytes(hall.at[pl.ds(0, TP - 1)], hall_sem.at[0])
    wait_bytes(urecv.at[0, pl.ds(0, TP - 1)], u_sem.at[0, 0])
    wait_bytes(urecv.at[1], u_sem.at[1, 0])


def tiles_rows(tiles, k):
    return tiles[:, k, :].astype(BF)


def per_device(hidden, queries, keys, values, lengths, weight, down, up, gain):
    slots = keys.shape[1]
    dma = pltpu.SemaphoreType.DMA
    return pl.pallas_call(
        kernel,
        name="decode",
        out_shape=(
            jax.ShapeDtypeStruct(queries.shape, BF),
            jax.ShapeDtypeStruct((STEPS, ROWS, 2 * HEAD), BF),
        ),
        in_specs=[pl.BlockSpec(memory_space=pl.ANY)] * 9,
        out_specs=(pl.BlockSpec(memory_space=pltpu.VMEM),) * 2,
        scratch_shapes=[
            pltpu.VMEM(hidden.shape, BF),
            pltpu.VMEM(queries.shape, BF),
            pltpu.VMEM(keys.shape, BF),
            pltpu.VMEM(values.shape, BF),
            pltpu.SMEM(lengths.shape, jnp.int32),
            pltpu.VMEM(weight.shape, BF),
            pltpu.VMEM(down.shape, BF),
            pltpu.VMEM(up.shape, BF),
            pltpu.VMEM(gain.shape, F32),
            pltpu.VMEM((TOKENS, KB * HEAD), F32),
            pltpu.VMEM((ROWS * QUERIES, HEAD), F32),
            pltpu.VMEM((ROWS * QUERIES, HEAD), F32),
            pltpu.VMEM((PLANE, 8, HEAD), F32),
            pltpu.VMEM((TP, KB, TOKENS, HEAD), BF),
            pltpu.VMEM((UP, TOKENS, HEAD), BF),
            pltpu.VMEM((KB - UP, TOKENS, HEAD), BF),
            pltpu.VMEM((KB, TOKENS, HEAD), BF),
            pltpu.VMEM((2, PLANE, 2 * HEAD), BF),
            pltpu.VMEM((TOKENS, HEAD), BF),
            pltpu.VMEM((2, TP, TOKENS, HEAD), BF),
            dma((7,)),
            dma((2, ROWS)),
            dma((2,)),
            dma((2,)),
            dma((2, 2)),
            dma((2, 2)),
            dma((2,)),
            dma((2, 2)),
        ],
        compiler_params=pltpu.CompilerParams(
            collective_id=0, has_side_effects=True, vmem_limit_bytes=32 * 1024 * 1024
        ),
    )(hidden, queries, keys, values, lengths, weight, down, up, gain)


def solution(mesh):
    return jax.shard_map(
        per_device,
        mesh=mesh,
        in_specs=(
            P(None, "group", "tp"),
            P(None, "group", "tp"),
            P("group", None, "tp"),
            P("group", None, "tp"),
            P("group"),
            P(None, "tp"),
            P("group", "tp"),
            P("group", "tp"),
            P(),
        ),
        out_specs=(P(None, "group", "tp"), P(None, "group", "tp")),
        check_vma=False,
    )
```

```python
import functools

import jax
import jax.numpy as jnp
from jax import lax
from jax.experimental import pallas as pl
from jax.experimental.pallas import tpu as pltpu
from jax.sharding import PartitionSpec as P

HEAD = 128
STEPS = 4
ROWS = 4
HEADS = 8
TOKENS = STEPS * ROWS
QUERIES = STEPS * HEADS
TP = 8
PLANE = 32
KB = 5
UP = 3

ADAPTER_SCALE = 2.0
NORM_EPS = 1e-06
MESH = pl.DeviceIdType.MESH
BF = jnp.bfloat16
F32 = jnp.float32


def dot(a, b):
    return jnp.dot(a, b, preferred_element_type=F32)


def dot_t(a, b):
    return lax.dot_general(a, b, (((1,), (1,)), ((), ())), preferred_element_type=F32)


def kernel(
    hidden_hbm, queries_hbm, keys_hbm, values_hbm, lengths_hbm, weight_hbm, down_hbm, up_hbm, gain_hbm,
    att_ref, ent_ref,
    hidden_v, queries_v, keys_v, values_v, lengths_s, weight_v, down_v, up_v, gain_v,
    hf, q32, o32, tiles, hall, relay_up, relay_down, partner, bbuf, usend, urecv,
    loc_sem, kv_sem, tile_sem, hall_sem, relay_sem, partner_sem, b_sem, u_sem,
):
    g = lax.axis_index("group")
    t = lax.axis_index("tp")
    xy, zh, c = g // 4, (g // 2) % 2, g % 2
    z = zh * 8 + t
    me = xy * 2 + c

    def at_z(where):
        where = where % 16
        return (xy * 4 + (where // 8) * 2 + c, where % 8)

    def in_plane(i):
        p = (me + 1 + i) % PLANE
        return ((p // 2) * 4 + zh * 2 + p % 2, t)

    def remote(src, dst, send, recv, to):
        return pltpu.make_async_remote_copy(
            src_ref=src, dst_ref=dst, send_sem=send, recv_sem=recv, device_id=to, device_id_type=MESH
        )

    def wait_bytes(ref, sem):
        pltpu.make_async_copy(ref, ref, sem).wait()

    small = [
        pltpu.make_async_copy(src, dst, loc_sem.at[i])
        for i, (src, dst) in enumerate(
            (
                (hidden_hbm, hidden_v),
                (down_hbm, down_v),
                (up_hbm, up_v),
                (queries_hbm, queries_v),
                (lengths_hbm, lengths_s),
                (gain_hbm, gain_v),
                (weight_hbm, weight_v),
            )
        )
    ]
    for copy in small[:6]:
        copy.start()
    barrier = pltpu.get_barrier_semaphore()

    def greet_plane(i, _):
        pl.semaphore_signal(barrier, inc=1, device_id=in_plane(i), device_id_type=MESH)
        return 0

    lax.fori_loop(0, PLANE - 1, greet_plane, 0)

    def greet_z(i, _):
        pl.semaphore_signal(barrier, inc=1, device_id=at_z(z + 1 + i), device_id_type=MESH)
        pl.semaphore_signal(barrier, inc=1, device_id=at_z(z + 15 - i), device_id_type=MESH)
        return 0

    lax.fori_loop(0, 4, greet_z, 0)

    kv = []
    for r in range(ROWS):
        kv.append(
            (
                pltpu.make_async_copy(keys_hbm.at[r], keys_v.at[r], kv_sem.at[0, r]),
                pltpu.make_async_copy(values_hbm.at[r], values_v.at[r], kv_sem.at[1, r]),
            )
        )
        kv[r][0].start()
        kv[r][1].start()
    small[6].start()

    small[0].wait()
    for s in range(STEPS):
        hf[s * ROWS : (s + 1) * ROWS, :] = hidden_v[s].astype(F32)
    for k in range(KB):
        hall[t, k] = hf[:, k * HEAD : (k + 1) * HEAD].astype(BF)
    small[1].wait()
    small[2].wait()
    down = down_v[...].astype(F32)
    up = up_v[...].astype(F32)
    for k in range(KB):
        tiles[me, k : k + 1, :] = down[:, k * HEAD : (k + 1) * HEAD]
    for k in range(2):
        tiles[me, KB + k : KB + k + 1, :] = up[:, k * HEAD : (k + 1) * HEAD]
    tiles[me, 7:8, :] = jnp.zeros((1, HEAD), F32)

    pl.semaphore_wait(barrier, PLANE - 1 + 8)

    first_up = remote(hall.at[t, pl.ds(0, UP)], relay_up, relay_sem.at[0, 0], relay_sem.at[0, 1], at_z(z + 4))
    first_down = remote(
        hall.at[t, pl.ds(UP, KB - UP)], relay_down, relay_sem.at[1, 0], relay_sem.at[1, 1], at_z(z + 12)
    )
    first_up.start()
    first_down.start()

    def send_tile(i, _):
        remote(tiles.at[me], tiles.at[me], tile_sem.at[0], tile_sem.at[1], in_plane(i)).start()
        return 0

    lax.fori_loop(0, PLANE - 1, send_tile, 0)

    def send_hidden(d):
        @pl.when(t + d < TP)
        def _():
            remote(hall.at[t], hall.at[t], hall_sem.at[0], hall_sem.at[1], (g, t + d)).start()

        @pl.when(t >= d)
        def _():
            remote(hall.at[t], hall.at[t], hall_sem.at[0], hall_sem.at[1], (g, t - d)).start()

    for d in range(1, 5):
        send_hidden(d)

    small[3].wait()
    for s in range(STEPS):
        for h in range(HEADS):
            q32[pl.ds(s * HEADS + h, ROWS, stride=QUERIES), :] = queries_v[
                s, :, h * HEAD : (h + 1) * HEAD
            ].astype(F32)
    small[4].wait()
    factor = HEAD ** (-0.5)

    def cached(r):
        kv[r][0].wait()
        q = q32[r * QUERIES : (r + 1) * QUERIES, :].astype(BF)
        scores = dot_t(q, keys_v[r]) * factor
        slot = lax.broadcasted_iota(jnp.int32, scores.shape, 1)
        scores = jnp.where(slot < lengths_s[r], scores, -jnp.inf)
        top = jnp.max(scores, axis=1, keepdims=True)
        p = jnp.exp(scores - top)
        total = jnp.sum(p, axis=1, keepdims=True)
        kv[r][1].wait()
        return top, total, dot(p.astype(BF), values_v[r])

    rows = [cached(0), cached(1)]

    first_up.wait_recv()
    second_up = remote(relay_up, partner.at[pl.ds(0, UP)], partner_sem.at[0, 0], partner_sem.at[0, 1], at_z(z + 4))
    second_up.start()
    first_down.wait_recv()
    second_down = remote(
        relay_down, partner.at[pl.ds(UP, KB - UP)], partner_sem.at[1, 0], partner_sem.at[1, 1], at_z(z + 12)
    )
    second_down.start()
    for d in range(5, 8):
        send_hidden(d)

    rows += [cached(2), cached(3)]

    wait_bytes(tiles.at[pl.ds(0, PLANE - 1)], tile_sem.at[1])
    a = []
    for k in range(KB):
        block = tiles_rows(tiles, k)
        a.append(jnp.concatenate([block] * 4, axis=0))
    a = jnp.concatenate(a, axis=1)
    bbuf[0, :, 0:HEAD] = tiles_rows(tiles, KB)
    bbuf[0, :, HEAD : 2 * HEAD] = tiles_rows(tiles, KB + 1)
    send_b = remote(bbuf.at[0], bbuf.at[1], b_sem.at[0], b_sem.at[1], at_z(z + 8))
    send_b.start()

    def parts(blocks):
        u = dot_t(jnp.concatenate(blocks, axis=1), a)
        high = u.astype(BF).astype(F32)
        rest = u - high
        mid = rest.astype(BF).astype(F32)
        low = (rest - mid).astype(BF).astype(F32)
        lane = lax.broadcasted_iota(jnp.int32, u.shape, 1)
        zero = jnp.zeros_like(u)
        packed = jnp.where(lane < 32, high, jnp.where(lane < 64, mid, jnp.where(lane < 96, low, zero)))
        return packed.astype(BF)

    urecv[0, t] = parts([hall[t, k] for k in range(KB)])

    def send_own(i, _):
        remote(urecv.at[0, t], urecv.at[0, t], u_sem.at[0, 0], u_sem.at[0, 1], (g, (t + 1 + i) % TP)).start()
        return 0

    lax.fori_loop(0, TP - 1, send_own, 0)

    second_up.wait_recv()
    second_down.wait_recv()
    usend[...] = parts([partner[k] for k in range(KB)])
    other = xy * 4 + (1 - zh) * 2 + c

    def send_cross(i, _):
        remote(usend, urecv.at[1, t], u_sem.at[1, 0], u_sem.at[1, 1], (other, (t + i) % TP)).start()
        return 0

    lax.fori_loop(0, TP, send_cross, 0)

    wait_bytes(hall.at[pl.ds(0, TP - 1)], hall_sem.at[1])
    small[6].wait()
    base = jnp.zeros((TOKENS, 2 * HEAD), F32)
    for i in range(TP):
        block = jnp.concatenate([hall[i, k] for k in range(KB)], axis=1)
        base = base + dot(block, weight_v[i * KB * HEAD : (i + 1) * KB * HEAD, :])

    top_c = jnp.concatenate([r[0] for r in rows], axis=0)
    total_c = jnp.concatenate([r[1] for r in rows], axis=0)
    acc_c = jnp.concatenate([r[2] for r in rows], axis=0)
    small[5].wait()
    gain = gain_v[...].reshape(1, HEAD)

    send_b.wait_recv()
    b_own = jnp.concatenate([bbuf[0]] * 4, axis=0)
    b_other = jnp.concatenate([bbuf[1]] * 4, axis=0)
    wait_bytes(urecv.at[0, pl.ds(0, TP - 1)], u_sem.at[0, 1])
    update = dot(urecv[0].reshape(TP * TOKENS, HEAD), b_own)
    wait_bytes(urecv.at[1], u_sem.at[1, 1])
    update = update + dot(urecv[1].reshape(TP * TOKENS, HEAD), b_other)
    update = jnp.sum(update.reshape(TP, TOKENS, 2 * HEAD), axis=0)
    projected = base + ADAPTER_SCALE * update

    raw = projected[:, 0:HEAD]
    value = projected[:, HEAD : 2 * HEAD]
    scale = lax.rsqrt(jnp.mean(raw * raw, axis=1, keepdims=True) + NORM_EPS)
    key = raw * scale * gain
    for s in range(STEPS):
        ent_ref[s, :, 0:HEAD] = key[s * ROWS : (s + 1) * ROWS].astype(BF)
        ent_ref[s, :, HEAD : 2 * HEAD] = value[s * ROWS : (s + 1) * ROWS].astype(BF)

    scores = dot_t(q32[...].astype(BF), key.astype(BF)) * factor
    qi = lax.broadcasted_iota(jnp.int32, scores.shape, 0)
    ki = lax.broadcasted_iota(jnp.int32, scores.shape, 1)
    seen = (ki % ROWS == qi // QUERIES) & (ki // ROWS <= (qi % QUERIES) // HEADS)
    scores = jnp.where(seen, scores, -jnp.inf)
    top = jnp.maximum(top_c, jnp.max(scores, axis=1, keepdims=True))
    p = jnp.exp(scores - top)
    carry = jnp.exp(top_c - top)
    total = carry * total_c + jnp.sum(p, axis=1, keepdims=True)
    result = (carry * acc_c + dot(p.astype(BF), value.astype(BF))) / total
    o32[...] = result
    for s in range(STEPS):
        for h in range(HEADS):
            att_ref[s, :, h * HEAD : (h + 1) * HEAD] = o32[
                pl.ds(s * HEADS + h, ROWS, stride=QUERIES), :
            ].astype(BF)

    first_up.wait_send()
    first_down.wait_send()
    second_up.wait_send()
    second_down.wait_send()
    send_b.wait_send()
    wait_bytes(tiles.at[pl.ds(0, PLANE - 1)], tile_sem.at[0])
    wait_bytes(hall.at[pl.ds(0, TP - 1)], hall_sem.at[0])
    wait_bytes(urecv.at[0, pl.ds(0, TP - 1)], u_sem.at[0, 0])
    wait_bytes(urecv.at[1], u_sem.at[1, 0])


def tiles_rows(tiles, k):
    return tiles[:, k, :].astype(BF)


def per_device(hidden, queries, keys, values, lengths, weight, down, up, gain):
    slots = keys.shape[1]
    dma = pltpu.SemaphoreType.DMA
    return pl.pallas_call(
        kernel,
        name="decode",
        out_shape=(
            jax.ShapeDtypeStruct(queries.shape, BF),
            jax.ShapeDtypeStruct((STEPS, ROWS, 2 * HEAD), BF),
        ),
        in_specs=[pl.BlockSpec(memory_space=pltpu.HBM)] * 9,
        out_specs=(pl.BlockSpec(memory_space=pltpu.VMEM),) * 2,
        scratch_shapes=[
            pltpu.VMEM(hidden.shape, BF),
            pltpu.VMEM(queries.shape, BF),
            pltpu.VMEM(keys.shape, BF),
            pltpu.VMEM(values.shape, BF),
            pltpu.SMEM(lengths.shape, jnp.int32),
            pltpu.VMEM(weight.shape, BF),
            pltpu.VMEM(down.shape, BF),
            pltpu.VMEM(up.shape, BF),
            pltpu.VMEM(gain.shape, F32),
            pltpu.VMEM((TOKENS, KB * HEAD), F32),
            pltpu.VMEM((ROWS * QUERIES, HEAD), F32),
            pltpu.VMEM((ROWS * QUERIES, HEAD), F32),
            pltpu.VMEM((PLANE, 8, HEAD), F32),
            pltpu.VMEM((TP, KB, TOKENS, HEAD), BF),
            pltpu.VMEM((UP, TOKENS, HEAD), BF),
            pltpu.VMEM((KB - UP, TOKENS, HEAD), BF),
            pltpu.VMEM((KB, TOKENS, HEAD), BF),
            pltpu.VMEM((2, PLANE, 2 * HEAD), BF),
            pltpu.VMEM((TOKENS, HEAD), BF),
            pltpu.VMEM((2, TP, TOKENS, HEAD), BF),
            dma((7,)),
            dma((2, ROWS)),
            dma((2,)),
            dma((2,)),
            dma((2, 2)),
            dma((2, 2)),
            dma((2,)),
            dma((2, 2)),
        ],
        compiler_params=pltpu.CompilerParams(
            collective_id=0, has_side_effects=True, vmem_limit_bytes=60 * 1024 * 1024
        ),
    )(hidden, queries, keys, values, lengths, weight, down, up, gain)


def solution(mesh):
    return jax.shard_map(
        per_device,
        mesh=mesh,
        in_specs=(
            P(None, "group", "tp"),
            P(None, "group", "tp"),
            P("group", None, "tp"),
            P("group", None, "tp"),
            P("group"),
            P(None, "tp"),
            P("group", "tp"),
            P("group", "tp"),
            P(),
        ),
        out_specs=(P(None, "group", "tp"), P(None, "group", "tp")),
        check_vma=False,
    )
```

```python
import jax
import jax.numpy as jnp
from jax import lax
from jax.experimental import pallas as pl
from jax.experimental.pallas import tpu as pltpu
from jax.sharding import PartitionSpec as P

HEAD = 128
STEPS = 4
ROWS = 4
HEADS = 8
TOKENS = STEPS * ROWS
QUERIES = STEPS * HEADS
TP = 8
PLANE = 32
KB = 5

ADAPTER_SCALE = 2.0
NORM_EPS = 1e-06
MESH = pl.DeviceIdType.MESH
BF = jnp.bfloat16
F32 = jnp.float32


def dot(a, b):
    return jnp.dot(a, b, preferred_element_type=F32)


def dot_t(a, b):
    return lax.dot_general(a, b, (((1,), (1,)), ((), ())), preferred_element_type=F32)


def kernel(
    hidden_hbm, queries_hbm, keys_hbm, values_hbm, lengths_hbm, weight_hbm, down_hbm, up_hbm, gain_hbm,
    att_ref, ent_ref,
    hidden_v, queries_v, keys_v, values_v, lengths_s, weight_v, down_v, up_v, gain_v,
    hf, rowf, q32, o32, tiles, hall, bbuf, usend, urecv,
    loc_sem, kv_sem, up_send, up_recv, down_send, down_recv, tile_send, tile_recv, b_sem, u_send, u_recv,
):
    g = lax.axis_index("group")
    t = lax.axis_index("tp")
    xy, zh, c = g // 4, (g // 2) % 2, g % 2
    z = zh * TP + t
    me = xy * 2 + c
    low, high = zh == 0, zh == 1

    def at_z(where):
        return (xy * 4 + (where // TP) * 2 + c, where % TP)

    def in_plane(i):
        p = (me + 1 + i) % PLANE
        return ((p // 2) * 4 + zh * 2 + p % 2, t)

    def remote(src, dst, send, recv, to):
        return pltpu.make_async_remote_copy(
            src_ref=src, dst_ref=dst, send_sem=send, recv_sem=recv, device_id=to, device_id_type=MESH
        )

    def wait_bytes(ref, sem):
        pltpu.make_async_copy(ref, ref, sem).wait()

    def times(start, stop, body):
        def step(i, _):
            body(i)
            return 0

        lax.fori_loop(start, stop, step, 0)

    small = [
        pltpu.make_async_copy(src, dst, loc_sem.at[i])
        for i, (src, dst) in enumerate(
            (
                (hidden_hbm, hidden_v),
                (down_hbm, down_v),
                (up_hbm, up_v),
                (queries_hbm, queries_v),
                (lengths_hbm, lengths_s),
                (gain_hbm, gain_v),
                (weight_hbm, weight_v),
            )
        )
    ]
    for copy in small[:6]:
        copy.start()

    barrier = pltpu.get_barrier_semaphore()

    def greet(to):
        pl.semaphore_signal(barrier, inc=1, device_id=to, device_id_type=MESH)

    @pl.when(z > 0)
    def _():
        greet(at_z(z - 1))

    @pl.when(z < 2 * TP - 1)
    def _():
        greet(at_z(z + 1))

    times(0, PLANE - 1, lambda i: greet(in_plane(i)))

    @pl.when(low)
    def _():
        times(t + 2, TP, lambda i: greet((g, i)))

    kv = []
    for r in range(ROWS):
        kv.append(
            (
                pltpu.make_async_copy(keys_hbm.at[r], keys_v.at[r], kv_sem.at[0, r]),
                pltpu.make_async_copy(values_hbm.at[r], values_v.at[r], kv_sem.at[1, r]),
            )
        )
        kv[r][0].start()
        kv[r][1].start()
    small[6].start()

    small[0].wait()
    for s in range(STEPS):
        hf[s * ROWS : (s + 1) * ROWS, :] = hidden_v[s].astype(F32)
    for k in range(KB):
        hall[z, k] = hf[:, k * HEAD : (k + 1) * HEAD].astype(BF)
    small[1].wait()
    small[2].wait()
    down = down_v[...].astype(F32)
    up = up_v[...].astype(F32)
    rowf[...] = jnp.zeros_like(rowf)
    for k in range(KB):
        rowf[k : k + 1, :] = down[:, k * HEAD : (k + 1) * HEAD]
    for k in range(2):
        rowf[KB + k : KB + k + 1, :] = up[:, k * HEAD : (k + 1) * HEAD]
    tiles[0, me] = rowf[0:8, :]
    hall[z, KB] = rowf[...].astype(BF)

    @pl.when(low)
    def _():
        pl.semaphore_wait(barrier, PLANE + t)

    @pl.when(high)
    def _():
        pl.semaphore_wait(barrier, PLANE + jnp.where(t < TP - 1, 1, 0))

    def up_copy(s):
        block = hall.at[(z - s + 2 * TP) % (2 * TP)]
        return remote(block, block, up_send.at[s], up_recv.at[s + 1], at_z((z + 1) % (2 * TP)))

    def down_copy(s):
        block = hall.at[(z + s) % (2 * TP), pl.ds(0, KB)]
        return remote(block, block, down_send.at[s], down_recv.at[s + 1], at_z((z + 2 * TP - 1) % (2 * TP)))

    def arrived_up(s):
        block = hall.at[(z - s + 2 * TP) % (2 * TP)]
        wait_bytes(block, up_recv.at[s])

    def arrived_down(s):
        block = hall.at[(z + s) % (2 * TP), pl.ds(0, KB)]
        wait_bytes(block, down_recv.at[s])

    sends_up = jnp.logical_or(low, t < TP - 1)
    sends_down = t > 0
    steps_up = jnp.where(low, t, TP)
    last_up = jnp.where(low, t + 1, jnp.where(t < TP - 1, TP, 0))
    steps_down = TP - 1 - t

    def tile_copy(which, i):
        return remote(
            tiles.at[which, me], tiles.at[which, me], tile_send.at[which], tile_recv.at[which], in_plane(i)
        )

    @pl.when(sends_up)
    def _():
        up_copy(0).start()

    times(0, PLANE - 1, lambda i: tile_copy(0, i).start())

    @pl.when(sends_down)
    def _():
        down_copy(0).start()

    def step_up(s):
        arrived_up(s)

        @pl.when(s < last_up)
        def _():
            up_copy(s).start()

    def step_down(s):
        arrived_down(s)

        @pl.when(sends_down)
        def _():
            down_copy(s).start()

    times(1, steps_up + 1, step_up)

    @pl.when(low)
    def _():
        times(1, steps_down + 1, step_down)

    def rows_of(which, k):
        return tiles[which, :, k, :].astype(BF)

    def factor_of(which):
        return jnp.concatenate(
            [jnp.concatenate([rows_of(which, k)] * 4, axis=0) for k in range(KB)], axis=1
        )

    def block_of(where):
        return jnp.concatenate([hall[where, k] for k in range(KB)], axis=1)

    def parts(block, a):
        u = dot_t(block, a)
        first = u.astype(BF).astype(F32)
        rest = u - first
        second = rest.astype(BF).astype(F32)
        third = (rest - second).astype(BF).astype(F32)
        lane = lax.broadcasted_iota(jnp.int32, u.shape, 1)
        zero = jnp.zeros_like(u)
        packed = jnp.where(lane < 32, first, jnp.where(lane < 64, second, jnp.where(lane < 96, third, zero)))
        return packed.astype(BF)

    def u_copy(src, which, where, send, to):
        return remote(src, urecv.at[which, where], u_send.at[send], u_recv.at[which], to)

    wait_bytes(tiles.at[0, pl.ds(0, PLANE - 1)], tile_recv.at[0])
    a_own = factor_of(0)

    @pl.when(high)
    def _():
        usend[...] = parts(block_of(t), a_own)
        times(0, TP, lambda i: u_copy(usend, 1, t, 1, (g - 2, i)).start())

    bbuf[0, :, 0:HEAD] = rows_of(0, KB)
    bbuf[0, :, HEAD : 2 * HEAD] = rows_of(0, KB + 1)

    def b_copy():
        return remote(bbuf.at[0], bbuf.at[1], b_sem.at[0], b_sem.at[1], at_z(z - TP))

    @pl.when(high)
    def _():
        b_copy().start()
        tiles[1, me] = hall[t, KB].astype(F32)[0:8]
        times(0, PLANE - 1, lambda i: tile_copy(1, i).start())

    urecv[0, t] = parts(block_of(z), a_own)

    def own_copy(which, send, i):
        return u_copy(urecv.at[which, t], which, t, send, (g, (t + 1 + i) % TP))

    @pl.when(low)
    def _():
        times(0, TP - 1, lambda i: own_copy(0, 0, i).start())

    small[3].wait()
    for s in range(STEPS):
        for h in range(HEADS):
            q32[pl.ds(s * HEADS + h, ROWS, stride=QUERIES), :] = queries_v[
                s, :, h * HEAD : (h + 1) * HEAD
            ].astype(F32)
    small[4].wait()
    factor = HEAD ** (-0.5)

    def cached(r):
        kv[r][0].wait()
        q = q32[r * QUERIES : (r + 1) * QUERIES, :].astype(BF)
        scores = dot_t(q, keys_v[r]) * factor
        slot = lax.broadcasted_iota(jnp.int32, scores.shape, 1)
        scores = jnp.where(slot < lengths_s[r], scores, -jnp.inf)
        top = jnp.max(scores, axis=1, keepdims=True)
        p = jnp.exp(scores - top)
        total = jnp.sum(p, axis=1, keepdims=True)
        kv[r][1].wait()
        return top, total, dot(p.astype(BF), values_v[r])

    rows = [cached(r) for r in range(ROWS)]
    top_c = jnp.concatenate([r[0] for r in rows], axis=0)
    total_c = jnp.concatenate([r[1] for r in rows], axis=0)
    acc_c = jnp.concatenate([r[2] for r in rows], axis=0)

    @pl.when(high)
    def _():
        times(1, steps_down + 1, step_down)
        times(0, TP - 1, lambda i: own_copy(0, 0, i).start())
        wait_bytes(tiles.at[1, pl.ds(0, PLANE - 1)], tile_recv.at[1])
        urecv[1, t] = parts(block_of(z), factor_of(1))
        times(0, TP - 1, lambda i: own_copy(1, 2, i).start())
        bbuf[1, :, 0:HEAD] = rows_of(1, KB)
        bbuf[1, :, HEAD : 2 * HEAD] = rows_of(1, KB + 1)

    small[6].wait()
    base = jnp.zeros((TOKENS, 2 * HEAD), F32)
    for i in range(TP):
        base = base + dot(block_of(zh * TP + i), weight_v[i * KB * HEAD : (i + 1) * KB * HEAD, :])
    small[5].wait()
    gain = gain_v[...].reshape(1, HEAD)

    def update(which):
        b = jnp.concatenate([bbuf[which]] * 4, axis=0)
        return dot(urecv[which].reshape(TP * TOKENS, HEAD), b)

    def fold(x):
        return ADAPTER_SCALE * jnp.sum(x.reshape(TP, TOKENS, 2 * HEAD), axis=0)

    wait_bytes(urecv.at[0, pl.ds(0, TP - 1)], u_recv.at[0])
    base = base + fold(update(0))

    @pl.when(low)
    def _():
        wait_bytes(urecv.at[1], u_recv.at[1])
        wait_bytes(bbuf.at[1], b_sem.at[1])

    @pl.when(high)
    def _():
        wait_bytes(urecv.at[1, pl.ds(0, TP - 1)], u_recv.at[1])

    projected = base + fold(update(1))

    raw = projected[:, 0:HEAD]
    value = projected[:, HEAD : 2 * HEAD]
    scale = lax.rsqrt(jnp.mean(raw * raw, axis=1, keepdims=True) + NORM_EPS)
    key = raw * scale * gain
    for s in range(STEPS):
        ent_ref[s, :, 0:HEAD] = key[s * ROWS : (s + 1) * ROWS].astype(BF)
        ent_ref[s, :, HEAD : 2 * HEAD] = value[s * ROWS : (s + 1) * ROWS].astype(BF)

    scores = dot_t(q32[...].astype(BF), key.astype(BF)) * factor
    qi = lax.broadcasted_iota(jnp.int32, scores.shape, 0)
    ki = lax.broadcasted_iota(jnp.int32, scores.shape, 1)
    seen = (ki % ROWS == qi // QUERIES) & (ki // ROWS <= (qi % QUERIES) // HEADS)
    scores = jnp.where(seen, scores, -jnp.inf)
    top = jnp.maximum(top_c, jnp.max(scores, axis=1, keepdims=True))
    p = jnp.exp(scores - top)
    carry = jnp.exp(top_c - top)
    total = carry * total_c + jnp.sum(p, axis=1, keepdims=True)
    o32[...] = (carry * acc_c + dot(p.astype(BF), value.astype(BF))) / total
    for s in range(STEPS):
        for h in range(HEADS):
            att_ref[s, :, h * HEAD : (h + 1) * HEAD] = o32[
                pl.ds(s * HEADS + h, ROWS, stride=QUERIES), :
            ].astype(BF)

    times(0, last_up, lambda s: up_copy(s).wait_send())

    @pl.when(sends_down)
    def _():
        times(0, steps_down + 1, lambda s: down_copy(s).wait_send())

    wait_bytes(tiles.at[0, pl.ds(0, PLANE - 1)], tile_send.at[0])
    wait_bytes(urecv.at[0, pl.ds(0, TP - 1)], u_send.at[0])

    @pl.when(high)
    def _():
        wait_bytes(tiles.at[1, pl.ds(0, PLANE - 1)], tile_send.at[1])
        wait_bytes(urecv.at[1], u_send.at[1])
        wait_bytes(urecv.at[1, pl.ds(0, TP - 1)], u_send.at[2])
        b_copy().wait_send()


def per_device(hidden, queries, keys, values, lengths, weight, down, up, gain):
    dma = pltpu.SemaphoreType.DMA
    return pl.pallas_call(
        kernel,
        name="decode",
        out_shape=(
            pltpu.VMEM(queries.shape, BF),
            pltpu.VMEM((STEPS, ROWS, 2 * HEAD), BF),
        ),
        in_specs=[pl.BlockSpec(memory_space=pltpu.HBM)] * 9,
        out_specs=(pl.BlockSpec(memory_space=pltpu.VMEM),) * 2,
        scratch_shapes=[
            pltpu.VMEM(hidden.shape, BF),
            pltpu.VMEM(queries.shape, BF),
            pltpu.VMEM(keys.shape, BF),
            pltpu.VMEM(values.shape, BF),
            pltpu.SMEM(lengths.shape, jnp.int32),
            pltpu.VMEM(weight.shape, BF),
            pltpu.VMEM(down.shape, BF),
            pltpu.VMEM(up.shape, BF),
            pltpu.VMEM(gain.shape, F32),
            pltpu.VMEM((TOKENS, KB * HEAD), F32),
            pltpu.VMEM((TOKENS, HEAD), F32),
            pltpu.VMEM((ROWS * QUERIES, HEAD), F32),
            pltpu.VMEM((ROWS * QUERIES, HEAD), F32),
            pltpu.VMEM((2, PLANE, 8, HEAD), F32),
            pltpu.VMEM((2 * TP, KB + 1, TOKENS, HEAD), BF),
            pltpu.VMEM((2, PLANE, 2 * HEAD), BF),
            pltpu.VMEM((TOKENS, HEAD), BF),
            pltpu.VMEM((2, TP, TOKENS, HEAD), BF),
            dma((7,)),
            dma((2, ROWS)),
            dma((TP + 1,)),
            dma((TP + 1,)),
            dma((TP + 1,)),
            dma((TP + 1,)),
            dma((2,)),
            dma((2,)),
            dma((2,)),
            dma((3,)),
            dma((2,)),
        ],
        compiler_params=pltpu.CompilerParams(
            collective_id=0, has_side_effects=True, vmem_limit_bytes=60 * 1024 * 1024
        ),
    )(hidden, queries, keys, values, lengths, weight, down, up, gain)


def solution(mesh):
    return jax.shard_map(
        per_device,
        mesh=mesh,
        in_specs=(
            P(None, "group", "tp"),
            P(None, "group", "tp"),
            P("group", None, "tp"),
            P("group", None, "tp"),
            P("group"),
            P(None, "tp"),
            P("group", "tp"),
            P("group", "tp"),
            P(),
        ),
        out_specs=(P(None, "group", "tp"), P(None, "group", "tp")),
        check_vma=False,
    )
```

```python
import jax
import jax.numpy as jnp
from jax import lax
from jax.experimental import pallas as pl
from jax.experimental.pallas import tpu as pltpu
from jax.sharding import PartitionSpec as P

HEAD = 128
STEPS = 4
ROWS = 4
HEADS = 8
TOKENS = STEPS * ROWS
QUERIES = STEPS * HEADS
TP = 8
QUAD = 4
PLANE = 32
KB = 5

ADAPTER_SCALE = 2.0
NORM_EPS = 1e-06
MESH = pl.DeviceIdType.MESH
BF = jnp.bfloat16
F32 = jnp.float32


def dot(a, b):
    return jnp.dot(a, b, preferred_element_type=F32)


def dot_t(a, b):
    return lax.dot_general(a, b, (((1,), (1,)), ((), ())), preferred_element_type=F32)


def kernel(
    hidden_hbm, queries_hbm, keys_hbm, values_hbm, lengths_hbm, weight_hbm, down_hbm, up_hbm, gain_hbm,
    att_ref, ent_ref,
    hidden_v, queries_v, keys_v, values_v, lengths_s, weight_v, down_v, up_v, gain_v,
    hf, rowf, q32, o32, tiles, hall, bbuf, usend, urecv,
    loc_sem, kv_sem, block_send, block_recv, quad_send, quad_recv, tile_send, tile_recv, b_sem, u_send, u_recv,
):
    g = lax.axis_index("group")
    t = lax.axis_index("tp")
    xy, zh, c = g // 4, (g // 2) % 2, g % 2
    z = zh * TP + t
    me = xy * 2 + c
    low, high = zh == 0, zh == 1

    def at_z(where):
        return (xy * 4 + (where // TP) * 2 + c, where % TP)

    def in_plane(i):
        p = jnp.where(i < me, i, i + 1)
        return ((p // 2) * 4 + zh * 2 + p % 2, t)

    def remote(src, dst, send, recv, to):
        return pltpu.make_async_remote_copy(
            src_ref=src, dst_ref=dst, send_sem=send, recv_sem=recv, device_id=to, device_id_type=MESH
        )

    def wait_bytes(ref, sem):
        pltpu.make_async_copy(ref, ref, sem).wait()

    def times(start, stop, body):
        def step(i, _):
            body(i)
            return 0

        lax.fori_loop(start, stop, step, 0)

    small = [
        pltpu.make_async_copy(src, dst, loc_sem.at[i])
        for i, (src, dst) in enumerate(
            (
                (hidden_hbm, hidden_v),
                (down_hbm, down_v),
                (up_hbm, up_v),
                (queries_hbm, queries_v),
                (lengths_hbm, lengths_s),
                (gain_hbm, gain_v),
                (weight_hbm, weight_v),
            )
        )
    ]
    for copy in small[:6]:
        copy.start()

    barrier = pltpu.get_barrier_semaphore()

    def greet(to):
        pl.semaphore_signal(barrier, inc=1, device_id=to, device_id_type=MESH)

    def greet_z(d):
        greet(at_z((z - d + 2 * TP) % (2 * TP)))

        @pl.when(z + d < 2 * TP)
        def _():
            greet(at_z(z + d))

    times(1, QUAD + 1, greet_z)
    times(0, PLANE - 1, lambda i: greet(in_plane(i)))

    kv = []
    for r in range(ROWS):
        kv.append(
            (
                pltpu.make_async_copy(keys_hbm.at[r], keys_v.at[r], kv_sem.at[0, r]),
                pltpu.make_async_copy(values_hbm.at[r], values_v.at[r], kv_sem.at[1, r]),
            )
        )
        kv[r][0].start()
        kv[r][1].start()
    small[6].start()

    small[0].wait()
    for s in range(STEPS):
        hf[s * ROWS : (s + 1) * ROWS, :] = hidden_v[s].astype(F32)
    for k in range(KB):
        hall[z, k] = hf[:, k * HEAD : (k + 1) * HEAD].astype(BF)
    small[1].wait()
    small[2].wait()
    down = down_v[...].astype(F32)
    up = up_v[...].astype(F32)
    rowf[...] = jnp.zeros_like(rowf)
    for k in range(KB):
        rowf[k : k + 1, :] = down[:, k * HEAD : (k + 1) * HEAD]
    for k in range(2):
        rowf[KB + k : KB + k + 1, :] = up[:, k * HEAD : (k + 1) * HEAD]
    tiles[0, me] = rowf[0:8, :]
    hall[z, KB] = rowf[...].astype(BF)

    @pl.when(low)
    def _():
        pl.semaphore_wait(barrier, PLANE - 1 + QUAD + jnp.minimum(t, QUAD))

    @pl.when(high)
    def _():
        pl.semaphore_wait(barrier, PLANE - 1 + 2 * QUAD)

    first_quad = t < QUAD
    above, below = (z + QUAD) % (2 * TP), (z + 2 * TP - QUAD) % (2 * TP)
    sends_up = jnp.logical_or(low, first_quad)
    sends_down = jnp.logical_not(first_quad)
    passes_on = low != first_quad

    def up_copy():
        return remote(hall.at[z], hall.at[z], block_send.at[0], block_recv.at[0], at_z(above))

    def down_copy():
        block = hall.at[z, pl.ds(0, KB)]
        return remote(block, block, block_send.at[1], block_recv.at[1], at_z(below))

    def pass_copy():
        return remote(hall.at[below], hall.at[below], block_send.at[2], block_recv.at[2], at_z(above))

    def from_below():
        wait_bytes(hall.at[below], block_recv.at[0])

    def from_above():
        wait_bytes(hall.at[above, pl.ds(0, KB)], block_recv.at[1])

    apart = jnp.where(first_quad, QUAD, -QUAD)
    corner = z - t % QUAD

    def quad_copy(which, j):
        where = z + which * apart
        block = hall.at[where, pl.ds(0, KB)]
        to = corner + (t + 1 + j) % QUAD
        return remote(block, block, quad_send.at[which, j], quad_recv.at[which, j], at_z(to))

    def quad_arrived(which, j):
        where = corner + (t + 2 * QUAD - 1 - j) % QUAD + which * apart
        wait_bytes(hall.at[where, pl.ds(0, KB)], quad_recv.at[which, j])

    def tile_copy(which, i):
        return remote(
            tiles.at[which, me], tiles.at[which, me], tile_send.at[which], tile_recv.at[which], in_plane(i)
        )

    def send_down():
        @pl.when(sends_down)
        def _():
            down_copy().start()

    @pl.when(low)
    def _():
        up_copy().start()
        send_down()

    times(0, PLANE - 1, lambda i: tile_copy(0, i).start())

    @pl.when(low)
    def _():
        times(0, QUAD - 1, lambda j: quad_copy(0, j).start())

        @pl.when(first_quad)
        def _():
            from_above()

        @pl.when(jnp.logical_not(first_quad))
        def _():
            from_below()
            pass_copy().start()

        times(0, QUAD - 1, lambda j: quad_copy(1, j).start())

    @pl.when(jnp.logical_and(high, first_quad))
    def _():
        from_below()
        pass_copy().start()

    def rows_of(which, k):
        return tiles[which, :, k, :].astype(BF)

    def factor_of(which):
        return jnp.concatenate(
            [jnp.concatenate([rows_of(which, k)] * 4, axis=0) for k in range(KB)], axis=1
        )

    def block_of(where):
        return jnp.concatenate([hall[where, k] for k in range(KB)], axis=1)

    def parts(block, a):
        u = dot_t(block, a)
        first = u.astype(BF).astype(F32)
        rest = u - first
        second = rest.astype(BF).astype(F32)
        third = (rest - second).astype(BF).astype(F32)
        lane = lax.broadcasted_iota(jnp.int32, u.shape, 1)
        zero = jnp.zeros_like(u)
        packed = jnp.where(lane < 32, first, jnp.where(lane < 64, second, jnp.where(lane < 96, third, zero)))
        return packed.astype(BF)

    def u_copy(src, which, where, send, to):
        return remote(src, urecv.at[which, where], u_send.at[send], u_recv.at[which], to)

    wait_bytes(tiles.at[0, pl.ds(0, PLANE - 1)], tile_recv.at[0])
    a_own = factor_of(0)

    @pl.when(high)
    def _():
        wait_bytes(hall.at[t], block_recv.at[2])
        usend[...] = parts(block_of(t), a_own)
        times(0, TP, lambda i: u_copy(usend, 1, t, 1, (g - 2, i)).start())

    bbuf[0, :, 0:HEAD] = rows_of(0, KB)
    bbuf[0, :, HEAD : 2 * HEAD] = rows_of(0, KB + 1)

    def b_copy():
        return remote(bbuf.at[0], bbuf.at[1], b_sem.at[0], b_sem.at[1], at_z(z - TP))

    @pl.when(high)
    def _():
        b_copy().start()
        tiles[1, me] = hall[t, KB].astype(F32)[0:8]
        times(0, PLANE - 1, lambda i: tile_copy(1, i).start())

        @pl.when(first_quad)
        def _():
            up_copy().start()

        send_down()
        times(0, QUAD - 1, lambda j: quad_copy(0, j).start())

    urecv[0, t] = parts(block_of(z), a_own)

    def own_copy(which, send, i):
        return u_copy(urecv.at[which, t], which, t, send, (g, (t + 1 + i) % TP))

    @pl.when(low)
    def _():
        times(0, TP - 1, lambda i: own_copy(0, 0, i).start())

    small[3].wait()
    for s in range(STEPS):
        for h in range(HEADS):
            q32[pl.ds(s * HEADS + h, ROWS, stride=QUERIES), :] = queries_v[
                s, :, h * HEAD : (h + 1) * HEAD
            ].astype(F32)
    small[4].wait()
    factor = HEAD ** (-0.5)

    def cached(r):
        kv[r][0].wait()
        q = q32[r * QUERIES : (r + 1) * QUERIES, :].astype(BF)
        scores = dot_t(q, keys_v[r]) * factor
        slot = lax.broadcasted_iota(jnp.int32, scores.shape, 1)
        scores = jnp.where(slot < lengths_s[r], scores, -jnp.inf)
        top = jnp.max(scores, axis=1, keepdims=True)
        p = jnp.exp(scores - top)
        total = jnp.sum(p, axis=1, keepdims=True)
        kv[r][1].wait()
        return top, total, dot(p.astype(BF), values_v[r])

    rows = [cached(r) for r in range(ROWS)]
    top_c = jnp.concatenate([r[0] for r in rows], axis=0)
    total_c = jnp.concatenate([r[1] for r in rows], axis=0)
    acc_c = jnp.concatenate([r[2] for r in rows], axis=0)

    @pl.when(high)
    def _():
        @pl.when(first_quad)
        def _():
            from_above()

        @pl.when(jnp.logical_not(first_quad))
        def _():
            from_below()

        times(0, QUAD - 1, lambda j: quad_copy(1, j).start())
        times(0, TP - 1, lambda i: own_copy(0, 0, i).start())
        wait_bytes(tiles.at[1, pl.ds(0, PLANE - 1)], tile_recv.at[1])
        urecv[1, t] = parts(block_of(z), factor_of(1))
        times(0, TP - 1, lambda i: own_copy(1, 2, i).start())
        bbuf[1, :, 0:HEAD] = rows_of(1, KB)
        bbuf[1, :, HEAD : 2 * HEAD] = rows_of(1, KB + 1)

    for which in range(2):
        times(0, QUAD - 1, lambda j, which=which: quad_arrived(which, j))
    small[6].wait()
    base = jnp.zeros((TOKENS, 2 * HEAD), F32)
    for i in range(TP):
        base = base + dot(block_of(zh * TP + i), weight_v[i * KB * HEAD : (i + 1) * KB * HEAD, :])
    small[5].wait()
    gain = gain_v[...].reshape(1, HEAD)

    def update(which):
        b = jnp.concatenate([bbuf[which]] * 4, axis=0)
        return dot(urecv[which].reshape(TP * TOKENS, HEAD), b)

    def fold(x):
        return ADAPTER_SCALE * jnp.sum(x.reshape(TP, TOKENS, 2 * HEAD), axis=0)

    wait_bytes(urecv.at[0, pl.ds(0, TP - 1)], u_recv.at[0])
    base = base + fold(update(0))

    @pl.when(low)
    def _():
        wait_bytes(urecv.at[1], u_recv.at[1])
        wait_bytes(bbuf.at[1], b_sem.at[1])

    @pl.when(high)
    def _():
        wait_bytes(urecv.at[1, pl.ds(0, TP - 1)], u_recv.at[1])

    projected = base + fold(update(1))

    raw = projected[:, 0:HEAD]
    value = projected[:, HEAD : 2 * HEAD]
    scale = lax.rsqrt(jnp.mean(raw * raw, axis=1, keepdims=True) + NORM_EPS)
    key = raw * scale * gain
    for s in range(STEPS):
        ent_ref[s, :, 0:HEAD] = key[s * ROWS : (s + 1) * ROWS].astype(BF)
        ent_ref[s, :, HEAD : 2 * HEAD] = value[s * ROWS : (s + 1) * ROWS].astype(BF)

    scores = dot_t(q32[...].astype(BF), key.astype(BF)) * factor
    qi = lax.broadcasted_iota(jnp.int32, scores.shape, 0)
    ki = lax.broadcasted_iota(jnp.int32, scores.shape, 1)
    seen = (ki % ROWS == qi // QUERIES) & (ki // ROWS <= (qi % QUERIES) // HEADS)
    scores = jnp.where(seen, scores, -jnp.inf)
    top = jnp.maximum(top_c, jnp.max(scores, axis=1, keepdims=True))
    p = jnp.exp(scores - top)
    carry = jnp.exp(top_c - top)
    total = carry * total_c + jnp.sum(p, axis=1, keepdims=True)
    o32[...] = (carry * acc_c + dot(p.astype(BF), value.astype(BF))) / total
    for s in range(STEPS):
        for h in range(HEADS):
            att_ref[s, :, h * HEAD : (h + 1) * HEAD] = o32[
                pl.ds(s * HEADS + h, ROWS, stride=QUERIES), :
            ].astype(BF)

    @pl.when(sends_up)
    def _():
        up_copy().wait_send()

    @pl.when(sends_down)
    def _():
        down_copy().wait_send()

    @pl.when(passes_on)
    def _():
        pass_copy().wait_send()

    for which in range(2):
        times(0, QUAD - 1, lambda j, which=which: quad_copy(which, j).wait_send())
    wait_bytes(tiles.at[0, pl.ds(0, PLANE - 1)], tile_send.at[0])
    wait_bytes(urecv.at[0, pl.ds(0, TP - 1)], u_send.at[0])

    @pl.when(high)
    def _():
        wait_bytes(tiles.at[1, pl.ds(0, PLANE - 1)], tile_send.at[1])
        wait_bytes(urecv.at[1], u_send.at[1])
        wait_bytes(urecv.at[1, pl.ds(0, TP - 1)], u_send.at[2])
        b_copy().wait_send()


def per_device(hidden, queries, keys, values, lengths, weight, down, up, gain):
    dma = pltpu.SemaphoreType.DMA
    return pl.pallas_call(
        kernel,
        name="decode",
        out_shape=(
            pltpu.VMEM(queries.shape, BF),
            pltpu.VMEM((STEPS, ROWS, 2 * HEAD), BF),
        ),
        in_specs=[pl.BlockSpec(memory_space=pltpu.HBM)] * 9,
        out_specs=(pl.BlockSpec(memory_space=pltpu.VMEM),) * 2,
        scratch_shapes=[
            pltpu.VMEM(hidden.shape, BF),
            pltpu.VMEM(queries.shape, BF),
            pltpu.VMEM(keys.shape, BF),
            pltpu.VMEM(values.shape, BF),
            pltpu.SMEM(lengths.shape, jnp.int32),
            pltpu.VMEM(weight.shape, BF),
            pltpu.VMEM(down.shape, BF),
            pltpu.VMEM(up.shape, BF),
            pltpu.VMEM(gain.shape, F32),
            pltpu.VMEM((TOKENS, KB * HEAD), F32),
            pltpu.VMEM((TOKENS, HEAD), F32),
            pltpu.VMEM((ROWS * QUERIES, HEAD), F32),
            pltpu.VMEM((ROWS * QUERIES, HEAD), F32),
            pltpu.VMEM((2, PLANE, 8, HEAD), F32),
            pltpu.VMEM((2 * TP, KB + 1, TOKENS, HEAD), BF),
            pltpu.VMEM((2, PLANE, 2 * HEAD), BF),
            pltpu.VMEM((TOKENS, HEAD), BF),
            pltpu.VMEM((2, TP, TOKENS, HEAD), BF),
            dma((7,)),
            dma((2, ROWS)),
            dma((3,)),
            dma((3,)),
            dma((2, QUAD - 1)),
            dma((2, QUAD - 1)),
            dma((2,)),
            dma((2,)),
            dma((2,)),
            dma((3,)),
            dma((2,)),
        ],
        compiler_params=pltpu.CompilerParams(
            collective_id=0, has_side_effects=True, vmem_limit_bytes=60 * 1024 * 1024
        ),
    )(hidden, queries, keys, values, lengths, weight, down, up, gain)


def solution(mesh):
    return jax.shard_map(
        per_device,
        mesh=mesh,
        in_specs=(
            P(None, "group", "tp"),
            P(None, "group", "tp"),
            P("group", None, "tp"),
            P("group", None, "tp"),
            P("group"),
            P(None, "tp"),
            P("group", "tp"),
            P("group", "tp"),
            P(),
        ),
        out_specs=(P(None, "group", "tp"), P(None, "group", "tp")),
        check_vma=False,
    )
```

```python
import jax
import jax.numpy as jnp
from jax import lax
from jax.experimental import pallas as pl
from jax.experimental.pallas import tpu as pltpu
from jax.sharding import PartitionSpec as P

HEAD = 128
STEPS = 4
ROWS = 4
HEADS = 8
TOKENS = STEPS * ROWS
QUERIES = STEPS * HEADS
TP = 8
QUAD = 4
PLANE = 32
KB = 5

ADAPTER_SCALE = 2.0
NORM_EPS = 1e-06
MESH = pl.DeviceIdType.MESH
BF = jnp.bfloat16
F32 = jnp.float32


def dot(a, b):
    return jnp.dot(a, b, preferred_element_type=F32)


def dot_t(a, b):
    return lax.dot_general(a, b, (((1,), (1,)), ((), ())), preferred_element_type=F32)


def kernel(
    hidden_hbm, queries_hbm, keys_hbm, values_hbm, lengths_hbm, weight_hbm, down_hbm, up_hbm, gain_hbm,
    o32, e32,
    hidden_v, queries_v, keys_v, values_v, lengths_s, weight_v, down_v, up_v, gain_v,
    hf, rowf, q32, tiles, hall, wrap, bbuf, usend, urecv,
    loc_sem, kv_sem, block_send, block_recv, quad_send, quad_recv, tile_send, tile_recv, b_sem, wrap_send, wrap_recv, u_send, u_recv,
):
    g = lax.axis_index("group")
    t = lax.axis_index("tp")
    xy, zh, c = g // 4, (g // 2) % 2, g % 2
    z = zh * TP + t
    me = xy * 2 + c
    low, high = zh == 0, zh == 1
    round_about = t >= TP - 2

    def at_z(where):
        return (xy * 4 + (where // TP) * 2 + c, where % TP)

    def in_plane(i):
        p = jnp.where(i < me, i, i + 1)
        return ((p // 2) * 4 + zh * 2 + p % 2, t)

    def remote(src, dst, send, recv, to):
        return pltpu.make_async_remote_copy(
            src_ref=src, dst_ref=dst, send_sem=send, recv_sem=recv, device_id=to, device_id_type=MESH
        )

    def wait_bytes(ref, sem):
        pltpu.make_async_copy(ref, ref, sem).wait()

    def times(start, stop, body):
        def step(i, _):
            body(i)
            return 0

        lax.fori_loop(start, stop, step, 0)

    small = [
        pltpu.make_async_copy(src, dst, loc_sem.at[i])
        for i, (src, dst) in enumerate(
            (
                (hidden_hbm, hidden_v),
                (down_hbm, down_v),
                (up_hbm, up_v),
                (queries_hbm, queries_v),
                (lengths_hbm, lengths_s),
                (gain_hbm, gain_v),
                (weight_hbm, weight_v),
            )
        )
    ]
    for copy in small[:6]:
        copy.start()

    barrier = pltpu.get_barrier_semaphore()

    def greet(to):
        pl.semaphore_signal(barrier, inc=1, device_id=to, device_id_type=MESH)

    def greet_z(d):
        greet(at_z((z - d + 2 * TP) % (2 * TP)))

        @pl.when(z + d < 2 * TP)
        def _():
            greet(at_z(z + d))

    times(1, QUAD + 1, greet_z)

    @pl.when(low)
    def _():
        greet(at_z(z + TP))

    @pl.when(z == 0)
    def _():
        greet(at_z(TP - 2))
        greet(at_z(TP - 1))

    @pl.when(z >= 2 * TP - 2)
    def _():
        greet(at_z(0))

    times(0, PLANE - 1, lambda i: greet(in_plane(i)))

    kv = []
    for r in range(ROWS):
        kv.append(
            (
                pltpu.make_async_copy(keys_hbm.at[r], keys_v.at[r], kv_sem.at[0, r]),
                pltpu.make_async_copy(values_hbm.at[r], values_v.at[r], kv_sem.at[1, r]),
            )
        )
        kv[r][0].start()
        kv[r][1].start()
    small[6].start()

    small[0].wait()
    for s in range(STEPS):
        hf[s * ROWS : (s + 1) * ROWS, :] = hidden_v[s].astype(F32)
    for k in range(KB):
        hall[z, k] = hf[:, k * HEAD : (k + 1) * HEAD].astype(BF)
    small[1].wait()
    small[2].wait()
    down = down_v[...].astype(F32)
    up = up_v[...].astype(F32)
    rowf[...] = jnp.zeros_like(rowf)
    for k in range(KB):
        rowf[k : k + 1, :] = down[:, k * HEAD : (k + 1) * HEAD]
    for k in range(2):
        rowf[KB + k : KB + k + 1, :] = up[:, k * HEAD : (k + 1) * HEAD]
    tiles[0, me] = rowf[0:8, :]
    hall[z, KB] = rowf[...].astype(BF)

    @pl.when(low)
    def _():
        extra = jnp.where(t == 0, 2, jnp.where(round_about, 1, 0))
        pl.semaphore_wait(barrier, PLANE - 1 + QUAD + jnp.minimum(t, QUAD) + extra)

    @pl.when(high)
    def _():
        pl.semaphore_wait(barrier, PLANE + 2 * QUAD)

    first_quad = t < QUAD
    above, below = (z + QUAD) % (2 * TP), (z + 2 * TP - QUAD) % (2 * TP)
    sends_up = jnp.logical_or(jnp.logical_and(low, jnp.logical_not(round_about)), jnp.logical_and(high, first_quad))
    sends_down = jnp.logical_not(first_quad)
    passes_low = jnp.logical_and(low, sends_down)
    passes_high = jnp.logical_and(high, t < TP - 2 - QUAD)

    def up_copy():
        return remote(hall.at[z], hall.at[z], block_send.at[0], block_recv.at[0], at_z(above))

    def down_copy():
        block = hall.at[z, pl.ds(0, KB)]
        return remote(block, block, block_send.at[1], block_recv.at[1], at_z(below))

    def pass_copy():
        return remote(hall.at[below], hall.at[below], block_send.at[2], block_recv.at[2], at_z(above))

    def round_copy():
        return remote(hall.at[z], wrap.at[t - (TP - 2)], wrap_send.at[0], wrap_recv.at[t - (TP - 2)], at_z(0))

    def wrap_copy(i):
        return remote(wrap.at[i], hall.at[TP - 2 + i], wrap_send.at[i], block_recv.at[2], at_z(2 * TP - 2 + i))

    def from_below():
        wait_bytes(hall.at[below], block_recv.at[0])

    def from_above():
        wait_bytes(hall.at[above, pl.ds(0, KB)], block_recv.at[1])

    apart = jnp.where(first_quad, QUAD, -QUAD)
    corner = z - t % QUAD

    def quad_copy(which, j):
        where = z + which * apart
        block = hall.at[where, pl.ds(0, KB)]
        to = corner + (t + 1 + j) % QUAD
        return remote(block, block, quad_send.at[which, j], quad_recv.at[which, j], at_z(to))

    def quad_arrived(which, j):
        where = corner + (t + 2 * QUAD - 1 - j) % QUAD + which * apart
        wait_bytes(hall.at[where, pl.ds(0, KB)], quad_recv.at[which, j])

    def tile_copy(which, i):
        return remote(
            tiles.at[which, me], tiles.at[which, me], tile_send.at[which], tile_recv.at[which], in_plane(i)
        )

    def send_down():
        @pl.when(sends_down)
        def _():
            down_copy().start()

    def b_copy():
        return remote(bbuf.at[0], bbuf.at[1], b_sem.at[0], b_sem.at[1], at_z(z - TP))

    @pl.when(low)
    def _():
        @pl.when(round_about)
        def _():
            round_copy().start()

        @pl.when(jnp.logical_not(round_about))
        def _():
            up_copy().start()

        send_down()

    times(0, PLANE - 1, lambda i: tile_copy(0, i).start())

    @pl.when(low)
    def _():
        times(0, QUAD - 1, lambda j: quad_copy(0, j).start())

        @pl.when(first_quad)
        def _():
            from_above()

        @pl.when(jnp.logical_not(first_quad))
        def _():
            from_below()
            pass_copy().start()

        times(0, QUAD - 1, lambda j: quad_copy(1, j).start())

    @pl.when(high)
    def _():
        send_down()

    @pl.when(passes_high)
    def _():
        from_below()
        pass_copy().start()

    @pl.when(jnp.logical_and(high, first_quad))
    def _():
        up_copy().start()

    @pl.when(z == 0)
    def _():
        for i in (0, 1):
            wait_bytes(wrap.at[i], wrap_recv.at[i])
            wrap_copy(i).start()

    def rows_of(which, k):
        return tiles[which, :, k, :].astype(BF)

    def factor_of(which):
        return jnp.concatenate(
            [jnp.concatenate([rows_of(which, k)] * 4, axis=0) for k in range(KB)], axis=1
        )

    def block_of(where):
        return jnp.concatenate([hall[where, k] for k in range(KB)], axis=1)

    def parts(block, a):
        u = dot_t(block, a)
        first = u.astype(BF).astype(F32)
        rest = u - first
        second = rest.astype(BF).astype(F32)
        third = (rest - second).astype(BF).astype(F32)
        lane = lax.broadcasted_iota(jnp.int32, u.shape, 1)
        zero = jnp.zeros_like(u)
        packed = jnp.where(lane < 32, first, jnp.where(lane < 64, second, jnp.where(lane < 96, third, zero)))
        return packed.astype(BF)

    def u_copy(src, which, where, send, to):
        return remote(src, urecv.at[which, where], u_send.at[send], u_recv.at[which], to)

    wait_bytes(tiles.at[0, pl.ds(0, PLANE - 1)], tile_recv.at[0])
    a_own = factor_of(0)

    for k in range(2):
        bbuf[0, :, k * HEAD : (k + 1) * HEAD] = rows_of(0, KB + k)

    @pl.when(high)
    def _():
        b_copy().start()
        wait_bytes(hall.at[t], block_recv.at[2])
        usend[...] = parts(block_of(t), a_own)
        times(0, TP, lambda i: u_copy(usend, 1, t, 1, (g - 2, i)).start())

    @pl.when(high)
    def _():
        tiles[1, me] = hall[t, KB].astype(F32)[0:8]
        times(0, PLANE - 1, lambda i: tile_copy(1, i).start())

        times(0, QUAD - 1, lambda j: quad_copy(0, j).start())

    urecv[0, t] = parts(block_of(z), a_own)

    def own_copy(which, send, i):
        return u_copy(urecv.at[which, t], which, t, send, (g, (t + 1 + i) % TP))

    @pl.when(low)
    def _():
        times(0, TP - 1, lambda i: own_copy(0, 0, i).start())

    small[3].wait()
    for s in range(STEPS):
        for h in range(HEADS):
            q32[pl.ds(s * HEADS + h, ROWS, stride=QUERIES), :] = queries_v[
                s, :, h * HEAD : (h + 1) * HEAD
            ].astype(F32)
    small[4].wait()
    factor = HEAD ** (-0.5)

    def cached(r):
        kv[r][0].wait()
        q = q32[r * QUERIES : (r + 1) * QUERIES, :].astype(BF)
        scores = dot_t(q, keys_v[r]) * factor
        slot = lax.broadcasted_iota(jnp.int32, scores.shape, 1)
        scores = jnp.where(slot < lengths_s[r], scores, -jnp.inf)
        top = jnp.max(scores, axis=1, keepdims=True)
        p = jnp.exp(scores - top)
        total = jnp.sum(p, axis=1, keepdims=True)
        kv[r][1].wait()
        return top, total, dot(p.astype(BF), values_v[r])

    rows = [cached(r) for r in range(ROWS)]
    top_c = jnp.concatenate([r[0] for r in rows], axis=0)
    total_c = jnp.concatenate([r[1] for r in rows], axis=0)
    acc_c = jnp.concatenate([r[2] for r in rows], axis=0)

    @pl.when(high)
    def _():
        @pl.when(first_quad)
        def _():
            from_above()

        @pl.when(jnp.logical_not(first_quad))
        def _():
            from_below()

        times(0, QUAD - 1, lambda j: quad_copy(1, j).start())
        times(0, TP - 1, lambda i: own_copy(0, 0, i).start())
        wait_bytes(tiles.at[1, pl.ds(0, PLANE - 1)], tile_recv.at[1])
        urecv[1, t] = parts(block_of(z), factor_of(1))
        times(0, TP - 1, lambda i: own_copy(1, 2, i).start())
        for k in range(2):
            bbuf[1, :, k * HEAD : (k + 1) * HEAD] = rows_of(1, KB + k)

    for which in range(2):
        times(0, QUAD - 1, lambda j, which=which: quad_arrived(which, j))
    small[6].wait()
    base = jnp.zeros((TOKENS, 2 * HEAD), F32)
    for i in range(TP):
        base = base + dot(block_of(zh * TP + i), weight_v[i * KB * HEAD : (i + 1) * KB * HEAD, :])
    small[5].wait()
    gain = gain_v[...].reshape(1, HEAD)

    def update(which):
        b = jnp.concatenate([bbuf[which]] * 4, axis=0)
        return dot(urecv[which].reshape(TP * TOKENS, HEAD), b)

    def fold(x):
        return ADAPTER_SCALE * jnp.sum(x.reshape(TP, TOKENS, 2 * HEAD), axis=0)

    wait_bytes(urecv.at[0, pl.ds(0, TP - 1)], u_recv.at[0])
    base = base + fold(update(0))

    @pl.when(low)
    def _():
        wait_bytes(bbuf.at[1], b_sem.at[1])
        wait_bytes(urecv.at[1], u_recv.at[1])

    @pl.when(high)
    def _():
        wait_bytes(urecv.at[1, pl.ds(0, TP - 1)], u_recv.at[1])

    projected = base + fold(update(1))

    raw = projected[:, 0:HEAD]
    value = projected[:, HEAD : 2 * HEAD]
    scale = lax.rsqrt(jnp.mean(raw * raw, axis=1, keepdims=True) + NORM_EPS)
    key = raw * scale * gain
    e32[:, 0:HEAD] = key
    e32[:, HEAD : 2 * HEAD] = value

    scores = dot_t(q32[...].astype(BF), key.astype(BF)) * factor
    qi = lax.broadcasted_iota(jnp.int32, scores.shape, 0)
    ki = lax.broadcasted_iota(jnp.int32, scores.shape, 1)
    seen = (ki % ROWS == qi // QUERIES) & (ki // ROWS <= (qi % QUERIES) // HEADS)
    scores = jnp.where(seen, scores, -jnp.inf)
    top = jnp.maximum(top_c, jnp.max(scores, axis=1, keepdims=True))
    p = jnp.exp(scores - top)
    carry = jnp.exp(top_c - top)
    total = carry * total_c + jnp.sum(p, axis=1, keepdims=True)
    o32[...] = (carry * acc_c + dot(p.astype(BF), value.astype(BF))) / total
    @pl.when(sends_up)
    def _():
        up_copy().wait_send()

    @pl.when(sends_down)
    def _():
        down_copy().wait_send()

    @pl.when(jnp.logical_or(passes_low, passes_high))
    def _():
        pass_copy().wait_send()

    @pl.when(jnp.logical_and(low, round_about))
    def _():
        round_copy().wait_send()

    @pl.when(z == 0)
    def _():
        wrap_copy(0).wait_send()
        wrap_copy(1).wait_send()

    for which in range(2):
        times(0, QUAD - 1, lambda j, which=which: quad_copy(which, j).wait_send())
    wait_bytes(tiles.at[0, pl.ds(0, PLANE - 1)], tile_send.at[0])
    wait_bytes(urecv.at[0, pl.ds(0, TP - 1)], u_send.at[0])

    @pl.when(high)
    def _():
        wait_bytes(urecv.at[1], u_send.at[1])
        wait_bytes(urecv.at[1, pl.ds(0, TP - 1)], u_send.at[2])
        b_copy().wait_send()
        wait_bytes(tiles.at[1, pl.ds(0, PLANE - 1)], tile_send.at[1])


def write_out(o32, e32, att_ref, ent_ref):
    for s in range(STEPS):
        ent_ref[s] = e32[s * ROWS : (s + 1) * ROWS, :].astype(BF)
        for h in range(HEADS):
            att_ref[s, :, h * HEAD : (h + 1) * HEAD] = o32[
                pl.ds(s * HEADS + h, ROWS, stride=QUERIES), :
            ].astype(BF)


def per_device(hidden, queries, keys, values, lengths, weight, down, up, gain):
    dma = pltpu.SemaphoreType.DMA
    attention, entries = pl.pallas_call(
        kernel,
        name="decode",
        out_shape=(
            pltpu.VMEM((ROWS * QUERIES, HEAD), F32),
            pltpu.VMEM((TOKENS, 2 * HEAD), F32),
        ),
        in_specs=[pl.BlockSpec(memory_space=pltpu.HBM)] * 9,
        out_specs=(pl.BlockSpec(memory_space=pltpu.VMEM),) * 2,
        scratch_shapes=[
            pltpu.VMEM(hidden.shape, BF),
            pltpu.VMEM(queries.shape, BF),
            pltpu.VMEM(keys.shape, BF),
            pltpu.VMEM(values.shape, BF),
            pltpu.SMEM(lengths.shape, jnp.int32),
            pltpu.VMEM(weight.shape, BF),
            pltpu.VMEM(down.shape, BF),
            pltpu.VMEM(up.shape, BF),
            pltpu.VMEM(gain.shape, F32),
            pltpu.VMEM((TOKENS, KB * HEAD), F32),
            pltpu.VMEM((TOKENS, HEAD), F32),
            pltpu.VMEM((ROWS * QUERIES, HEAD), F32),
            pltpu.VMEM((2, PLANE, 8, HEAD), F32),
            pltpu.VMEM((2 * TP, KB + 1, TOKENS, HEAD), BF),
            pltpu.VMEM((2, KB + 1, TOKENS, HEAD), BF),
            pltpu.VMEM((2, PLANE, 2 * HEAD), BF),
            pltpu.VMEM((TOKENS, HEAD), BF),
            pltpu.VMEM((2, TP, TOKENS, HEAD), BF),
            dma((7,)),
            dma((2, ROWS)),
            dma((3,)),
            dma((3,)),
            dma((2, QUAD - 1)),
            dma((2, QUAD - 1)),
            dma((2,)),
            dma((2,)),
            dma((2,)),
            dma((2,)),
            dma((2,)),
            dma((3,)),
            dma((2,)),
        ],
        compiler_params=pltpu.CompilerParams(
            collective_id=0, has_side_effects=True, vmem_limit_bytes=60 * 1024 * 1024
        ),
    )(hidden, queries, keys, values, lengths, weight, down, up, gain)
    return pl.pallas_call(
        write_out,
        name="write_out",
        out_shape=(
            jax.ShapeDtypeStruct(queries.shape, BF),
            jax.ShapeDtypeStruct((STEPS, ROWS, 2 * HEAD), BF),
        ),
        in_specs=[pl.BlockSpec(memory_space=pltpu.VMEM)] * 2,
        out_specs=(pl.BlockSpec(memory_space=pltpu.VMEM),) * 2,
        compiler_params=pltpu.CompilerParams(vmem_limit_bytes=2 * 1024 * 1024),
    )(attention, entries)


def solution(mesh):
    return jax.shard_map(
        per_device,
        mesh=mesh,
        in_specs=(
            P(None, "group", "tp"),
            P(None, "group", "tp"),
            P("group", None, "tp"),
            P("group", None, "tp"),
            P("group"),
            P(None, "tp"),
            P("group", "tp"),
            P("group", "tp"),
            P(),
        ),
        out_specs=(P(None, "group", "tp"), P(None, "group", "tp")),
        check_vma=False,
    )
```

```python
import jax
import jax.numpy as jnp
from jax import lax
from jax.experimental import pallas as pl
from jax.experimental.pallas import tpu as pltpu
from jax.sharding import PartitionSpec as P

HEAD = 128
STEPS = 4
ROWS = 4
HEADS = 8
TOKENS = STEPS * ROWS
QUERIES = STEPS * HEADS
TP = 8
QUAD = 4
PLANE = 32
KB = 5

ADAPTER_SCALE = 2.0
NORM_EPS = 1e-06
MESH = pl.DeviceIdType.MESH
BF = jnp.bfloat16
F32 = jnp.float32


def dot(a, b):
    return jnp.dot(a, b, preferred_element_type=F32)


def dot_t(a, b):
    return lax.dot_general(a, b, (((1,), (1,)), ((), ())), preferred_element_type=F32)


def kernel(
    hidden_hbm, queries_hbm, keys_hbm, values_hbm, lengths_hbm, weight_hbm, down_hbm, up_hbm, gain_hbm,
    o32, e32,
    hidden_v, queries_v, keys_v, values_v, lengths_s, weight_v, down_v, up_v, gain_v,
    hf, rowf, q32, acc32, top32, total32, tiles, hall, detour, bbuf, usend, urecv,
    loc_sem, kv_sem, block_send, block_recv, quad_send, quad_recv, tile_send, tile_recv, b_sem, detour_send, detour_recv, u_send, u_recv,
):
    g = lax.axis_index("group")
    t = lax.axis_index("tp")
    xy, zh, c = g // 4, (g // 2) % 2, g % 2
    z = zh * TP + t
    me = xy * 2 + c
    low, high = zh == 0, zh == 1

    def at_z(where):
        return (xy * 4 + (where // TP) * 2 + c, where % TP)

    def in_plane(i):
        p = jnp.where(i < me, i, i + 1)
        return ((p // 2) * 4 + zh * 2 + p % 2, t)

    def remote(src, dst, send, recv, to):
        return pltpu.make_async_remote_copy(
            src_ref=src, dst_ref=dst, send_sem=send, recv_sem=recv, device_id=to, device_id_type=MESH
        )

    def wait_bytes(ref, sem):
        pltpu.make_async_copy(ref, ref, sem).wait()

    def times(start, stop, body):
        def step(i, _):
            body(i)
            return 0

        lax.fori_loop(start, stop, step, 0)

    small = [
        pltpu.make_async_copy(src, dst, loc_sem.at[i])
        for i, (src, dst) in enumerate(
            (
                (hidden_hbm, hidden_v),
                (down_hbm, down_v),
                (up_hbm, up_v),
                (queries_hbm, queries_v),
                (lengths_hbm, lengths_s),
                (gain_hbm, gain_v),
                (weight_hbm, weight_v),
            )
        )
    ]
    for copy in small[:6]:
        copy.start()

    barrier = pltpu.get_barrier_semaphore()

    def greet(to):
        pl.semaphore_signal(barrier, inc=1, device_id=to, device_id_type=MESH)

    def greet_z(d):
        @pl.when(jnp.logical_not(jnp.logical_and(z == TP, d == QUAD)))
        def _():
            greet(at_z((z - d + 2 * TP) % (2 * TP)))

        @pl.when(z + d < 2 * TP)
        def _():
            greet(at_z(z + d))

    times(1, QUAD + 1, greet_z)

    @pl.when(low)
    def _():
        greet(at_z(z + TP))

    @pl.when(jnp.logical_or(z == 5, z == 12))
    def _():
        greet(at_z(z - 5))

    @pl.when(z >= TP + 5)
    def _():
        greet(at_z(z - TP))

    times(0, PLANE - 1, lambda i: greet(in_plane(i)))

    kv = []
    for r in range(ROWS):
        kv.append(
            (
                pltpu.make_async_copy(keys_hbm.at[r], keys_v.at[r], kv_sem.at[0, r]),
                pltpu.make_async_copy(values_hbm.at[r], values_v.at[r], kv_sem.at[1, r]),
            )
        )
        kv[r][0].start()
        kv[r][1].start()
    small[6].start()

    small[0].wait()
    for s in range(STEPS):
        hf[s * ROWS : (s + 1) * ROWS, :] = hidden_v[s].astype(F32)
    for k in range(KB):
        hall[z, k] = hf[:, k * HEAD : (k + 1) * HEAD].astype(BF)
    small[1].wait()
    small[2].wait()
    down = down_v[...].astype(F32)
    up = up_v[...].astype(F32)
    rowf[...] = jnp.zeros_like(rowf)
    for k in range(KB):
        rowf[k : k + 1, :] = down[:, k * HEAD : (k + 1) * HEAD]
    for k in range(2):
        rowf[KB + k : KB + k + 1, :] = up[:, k * HEAD : (k + 1) * HEAD]
    tiles[0, me] = rowf[0:8, :]
    hall[z, KB] = rowf[...].astype(BF)

    @pl.when(low)
    def _():
        extra = jnp.where(t == 4, -1, jnp.where(t == 7, 2, jnp.where(jnp.logical_or(t == 0, t > 4), 1, 0)))
        pl.semaphore_wait(barrier, PLANE - 1 + QUAD + jnp.minimum(t, QUAD) + extra)

    @pl.when(high)
    def _():
        pl.semaphore_wait(barrier, PLANE + 2 * QUAD)

    first_quad = t < QUAD
    above, below = (z + QUAD) % (2 * TP), (z + 2 * TP - QUAD) % (2 * TP)
    sends_up = first_quad
    sends_down = jnp.logical_not(first_quad)
    passes = jnp.logical_and(z >= 5, z < TP)
    detours = jnp.logical_and(low, t % 4 == 0)
    direct = jnp.logical_and(low, t > 4)

    def up_copy():
        return remote(hall.at[z], hall.at[z], block_send.at[0], block_recv.at[0], at_z(above))

    def down_copy():
        block = hall.at[z, pl.ds(0, KB)]
        return remote(block, block, block_send.at[1], block_recv.at[1], at_z(below))

    def pass_copy():
        return remote(hall.at[below], hall.at[below], block_send.at[2], block_recv.at[2], at_z(above))

    def direct_copy():
        return remote(hall.at[z], hall.at[z], block_send.at[0], block_recv.at[2], at_z((z + TP) % (2 * TP)))

    def detour_copy():
        to = jnp.where(t == 0, 5, 7)
        return remote(hall.at[z], detour, detour_send.at[0], detour_recv, at_z(to))

    def detour_on():
        owner = jnp.where(t == 5, 0, 4)
        return remote(detour, hall.at[owner], detour_send.at[1], block_recv.at[2], at_z(owner + TP))

    def send_on():
        wait_bytes(detour, detour_recv)
        detour_on().start()

    def from_below():
        wait_bytes(hall.at[below], block_recv.at[0])

    def from_above():
        wait_bytes(hall.at[above, pl.ds(0, KB)], block_recv.at[1])

    apart = jnp.where(first_quad, QUAD, -QUAD)
    corner = z - t % QUAD

    def quad_copy(which, j):
        where = z + which * apart
        block = hall.at[where, pl.ds(0, KB)]
        to = corner + (t + 1 + j) % QUAD
        return remote(block, block, quad_send.at[which, j], quad_recv.at[which, j], at_z(to))

    def quad_arrived(which, j):
        where = corner + (t + 2 * QUAD - 1 - j) % QUAD + which * apart
        wait_bytes(hall.at[where, pl.ds(0, KB)], quad_recv.at[which, j])

    def tile_copy(which, i):
        return remote(
            tiles.at[which, me], tiles.at[which, me], tile_send.at[which], tile_recv.at[which], in_plane(i)
        )

    def send_down():
        @pl.when(sends_down)
        def _():
            down_copy().start()

    def b_copy():
        return remote(bbuf.at[0], bbuf.at[1], b_sem.at[0], b_sem.at[1], at_z(z - TP))

    @pl.when(low)
    def _():
        @pl.when(detours)
        def _():
            detour_copy().start()

        @pl.when(direct)
        def _():
            direct_copy().start()

        @pl.when(sends_up)
        def _():
            up_copy().start()

        send_down()

    times(0, PLANE - 1, lambda i: tile_copy(0, i).start())

    @pl.when(low)
    def _():
        times(0, QUAD - 1, lambda j: quad_copy(0, j).start())

        @pl.when(first_quad)
        def _():
            from_above()

        @pl.when(t == 7)
        def _():
            send_on()

        @pl.when(jnp.logical_not(first_quad))
        def _():
            from_below()

            @pl.when(passes)
            def _():
                pass_copy().start()

        @pl.when(t == 5)
        def _():
            send_on()

        times(0, QUAD - 1, lambda j: quad_copy(1, j).start())

    @pl.when(high)
    def _():
        send_down()

    @pl.when(jnp.logical_and(high, first_quad))
    def _():
        up_copy().start()

    def rows_of(which, k):
        return tiles[which, :, k, :].astype(BF)

    def factor_of(which):
        return jnp.concatenate(
            [jnp.concatenate([rows_of(which, k)] * 4, axis=0) for k in range(KB)], axis=1
        )

    def block_of(where):
        return jnp.concatenate([hall[where, k] for k in range(KB)], axis=1)

    def parts(block, a):
        u = dot_t(block, a)
        first = u.astype(BF).astype(F32)
        rest = u - first
        second = rest.astype(BF).astype(F32)
        third = (rest - second).astype(BF).astype(F32)
        lane = lax.broadcasted_iota(jnp.int32, u.shape, 1)
        zero = jnp.zeros_like(u)
        packed = jnp.where(lane < 32, first, jnp.where(lane < 64, second, jnp.where(lane < 96, third, zero)))
        return packed.astype(BF)

    def u_copy(src, which, where, send, to):
        return remote(src, urecv.at[which, where], u_send.at[send], u_recv.at[which], to)

    wait_bytes(tiles.at[0, pl.ds(0, PLANE - 1)], tile_recv.at[0])
    a_own = factor_of(0)

    for k in range(2):
        bbuf[0, :, k * HEAD : (k + 1) * HEAD] = rows_of(0, KB + k)

    @pl.when(high)
    def _():
        b_copy().start()
        wait_bytes(hall.at[t], block_recv.at[2])
        usend[...] = parts(block_of(t), a_own)
        times(0, TP, lambda i: u_copy(usend, 1, t, 1, (g - 2, i)).start())

    @pl.when(high)
    def _():
        tiles[1, me] = hall[t, KB].astype(F32)[0:8]
        times(0, PLANE - 1, lambda i: tile_copy(1, i).start())

        times(0, QUAD - 1, lambda j: quad_copy(0, j).start())

    urecv[0, t] = parts(block_of(z), a_own)

    def own_copy(which, send, i):
        return u_copy(urecv.at[which, t], which, t, send, (g, (t + 1 + i) % TP))

    @pl.when(low)
    def _():
        times(0, TP - 1, lambda i: own_copy(0, 0, i).start())

    small[3].wait()
    for s in range(STEPS):
        for h in range(HEADS):
            q32[pl.ds(s * HEADS + h, ROWS, stride=QUERIES), :] = queries_v[
                s, :, h * HEAD : (h + 1) * HEAD
            ].astype(F32)
    small[4].wait()
    factor = HEAD ** (-0.5)

    def cached(r):
        wait_bytes(keys_v.at[r], kv_sem.at[0, r])
        own = pl.ds(pl.multiple_of(r * QUERIES, QUERIES), QUERIES)
        scores = dot_t(q32[own, :].astype(BF), keys_v[r]) * factor
        slot = lax.broadcasted_iota(jnp.int32, scores.shape, 1)
        scores = jnp.where(slot < lengths_s[r], scores, -jnp.inf)
        top = jnp.max(scores, axis=1, keepdims=True)
        p = jnp.exp(scores - top)
        total = jnp.sum(p, axis=1, keepdims=True)
        wait_bytes(values_v.at[r], kv_sem.at[1, r])
        acc32[own, :] = dot(p.astype(BF), values_v[r])
        top32[own, :] = jnp.broadcast_to(top, (QUERIES, HEAD))
        total32[own, :] = jnp.broadcast_to(total, (QUERIES, HEAD))

    times(0, ROWS, cached)

    @pl.when(high)
    def _():
        @pl.when(first_quad)
        def _():
            from_above()

        @pl.when(jnp.logical_not(first_quad))
        def _():
            from_below()

        times(0, QUAD - 1, lambda j: quad_copy(1, j).start())
        times(0, TP - 1, lambda i: own_copy(0, 0, i).start())
        wait_bytes(tiles.at[1, pl.ds(0, PLANE - 1)], tile_recv.at[1])
        urecv[1, t] = parts(block_of(z), factor_of(1))
        times(0, TP - 1, lambda i: own_copy(1, 2, i).start())
        for k in range(2):
            bbuf[1, :, k * HEAD : (k + 1) * HEAD] = rows_of(1, KB + k)

    for which in range(2):
        times(0, QUAD - 1, lambda j, which=which: quad_arrived(which, j))
    small[6].wait()

    def project(i, sofar):
        depth = KB * HEAD
        return sofar + dot(block_of(zh * TP + i), weight_v[pl.ds(pl.multiple_of(i * depth, depth), depth), :])

    base = lax.fori_loop(0, TP, project, jnp.zeros((TOKENS, 2 * HEAD), F32))
    small[5].wait()
    gain = gain_v[...].reshape(1, HEAD)

    def update(which):
        b = jnp.concatenate([bbuf[which]] * 4, axis=0)
        return dot(urecv[which].reshape(TP * TOKENS, HEAD), b)

    def fold(x):
        return ADAPTER_SCALE * jnp.sum(x.reshape(TP, TOKENS, 2 * HEAD), axis=0)

    wait_bytes(urecv.at[0, pl.ds(0, TP - 1)], u_recv.at[0])
    base = base + fold(update(0))

    @pl.when(low)
    def _():
        wait_bytes(bbuf.at[1], b_sem.at[1])
        wait_bytes(urecv.at[1], u_recv.at[1])

    @pl.when(high)
    def _():
        wait_bytes(urecv.at[1, pl.ds(0, TP - 1)], u_recv.at[1])

    projected = base + fold(update(1))

    raw = projected[:, 0:HEAD]
    value = projected[:, HEAD : 2 * HEAD]
    scale = lax.rsqrt(jnp.mean(raw * raw, axis=1, keepdims=True) + NORM_EPS)
    key = raw * scale * gain
    e32[:, 0:HEAD] = key
    e32[:, HEAD : 2 * HEAD] = value

    scores = dot_t(q32[...].astype(BF), key.astype(BF)) * factor
    qi = lax.broadcasted_iota(jnp.int32, scores.shape, 0)
    ki = lax.broadcasted_iota(jnp.int32, scores.shape, 1)
    seen = (ki % ROWS == qi // QUERIES) & (ki // ROWS <= (qi % QUERIES) // HEADS)
    scores = jnp.where(seen, scores, -jnp.inf)
    top_c = top32[:, 0:1]
    top = jnp.maximum(top_c, jnp.max(scores, axis=1, keepdims=True))
    p = jnp.exp(scores - top)
    carry = jnp.exp(top_c - top)
    total = carry * total32[:, 0:1] + jnp.sum(p, axis=1, keepdims=True)
    o32[...] = (carry * acc32[...] + dot(p.astype(BF), value.astype(BF))) / total

    @pl.when(sends_up)
    def _():
        up_copy().wait_send()

    @pl.when(sends_down)
    def _():
        down_copy().wait_send()

    @pl.when(passes)
    def _():
        pass_copy().wait_send()

    @pl.when(detours)
    def _():
        detour_copy().wait_send()

    @pl.when(jnp.logical_or(z == 5, z == 7))
    def _():
        detour_on().wait_send()

    @pl.when(direct)
    def _():
        direct_copy().wait_send()

    for which in range(2):
        times(0, QUAD - 1, lambda j, which=which: quad_copy(which, j).wait_send())
    wait_bytes(tiles.at[0, pl.ds(0, PLANE - 1)], tile_send.at[0])
    wait_bytes(urecv.at[0, pl.ds(0, TP - 1)], u_send.at[0])

    @pl.when(high)
    def _():
        wait_bytes(urecv.at[1], u_send.at[1])
        wait_bytes(urecv.at[1, pl.ds(0, TP - 1)], u_send.at[2])
        b_copy().wait_send()
        wait_bytes(tiles.at[1, pl.ds(0, PLANE - 1)], tile_send.at[1])


def write_out(o32, e32, att_ref, ent_ref):
    for s in range(STEPS):
        ent_ref[s] = e32[s * ROWS : (s + 1) * ROWS, :].astype(BF)
        for h in range(HEADS):
            att_ref[s, :, h * HEAD : (h + 1) * HEAD] = o32[
                pl.ds(s * HEADS + h, ROWS, stride=QUERIES), :
            ].astype(BF)


def per_device(hidden, queries, keys, values, lengths, weight, down, up, gain):
    dma = pltpu.SemaphoreType.DMA
    attention, entries = pl.pallas_call(
        kernel,
        name="decode",
        out_shape=(
            pltpu.VMEM((ROWS * QUERIES, HEAD), F32),
            pltpu.VMEM((TOKENS, 2 * HEAD), F32),
        ),
        in_specs=[pl.BlockSpec(memory_space=pltpu.HBM)] * 9,
        out_specs=(pl.BlockSpec(memory_space=pltpu.VMEM),) * 2,
        scratch_shapes=[
            pltpu.VMEM(hidden.shape, BF),
            pltpu.VMEM(queries.shape, BF),
            pltpu.VMEM(keys.shape, BF),
            pltpu.VMEM(values.shape, BF),
            pltpu.SMEM(lengths.shape, jnp.int32),
            pltpu.VMEM(weight.shape, BF),
            pltpu.VMEM(down.shape, BF),
            pltpu.VMEM(up.shape, BF),
            pltpu.VMEM(gain.shape, F32),
            pltpu.VMEM((TOKENS, KB * HEAD), F32),
            pltpu.VMEM((TOKENS, HEAD), F32),
            pltpu.VMEM((ROWS * QUERIES, HEAD), F32),
            pltpu.VMEM((ROWS * QUERIES, HEAD), F32),
            pltpu.VMEM((ROWS * QUERIES, HEAD), F32),
            pltpu.VMEM((ROWS * QUERIES, HEAD), F32),
            pltpu.VMEM((2, PLANE, 8, HEAD), F32),
            pltpu.VMEM((2 * TP, KB + 1, TOKENS, HEAD), BF),
            pltpu.VMEM((KB + 1, TOKENS, HEAD), BF),
            pltpu.VMEM((2, PLANE, 2 * HEAD), BF),
            pltpu.VMEM((TOKENS, HEAD), BF),
            pltpu.VMEM((2, TP, TOKENS, HEAD), BF),
            dma((7,)),
            dma((2, ROWS)),
            dma((3,)),
            dma((3,)),
            dma((2, QUAD - 1)),
            dma((2, QUAD - 1)),
            dma((2,)),
            dma((2,)),
            dma((2,)),
            dma((2,)),
            dma,
            dma((3,)),
            dma((2,)),
        ],
        compiler_params=pltpu.CompilerParams(
            collective_id=0, has_side_effects=True, vmem_limit_bytes=60 * 1024 * 1024
        ),
    )(hidden, queries, keys, values, lengths, weight, down, up, gain)
    return pl.pallas_call(
        write_out,
        name="write_out",
        out_shape=(
            jax.ShapeDtypeStruct(queries.shape, BF),
            jax.ShapeDtypeStruct((STEPS, ROWS, 2 * HEAD), BF),
        ),
        in_specs=[pl.BlockSpec(memory_space=pltpu.VMEM)] * 2,
        out_specs=(pl.BlockSpec(memory_space=pltpu.VMEM),) * 2,
        compiler_params=pltpu.CompilerParams(vmem_limit_bytes=2 * 1024 * 1024),
    )(attention, entries)


def solution(mesh):
    return jax.shard_map(
        per_device,
        mesh=mesh,
        in_specs=(
            P(None, "group", "tp"),
            P(None, "group", "tp"),
            P("group", None, "tp"),
            P("group", None, "tp"),
            P("group"),
            P(None, "tp"),
            P("group", "tp"),
            P("group", "tp"),
            P(),
        ),
        out_specs=(P(None, "group", "tp"), P(None, "group", "tp")),
        check_vma=False,
    )
```

```python
import jax
import jax.numpy as jnp
from jax import lax
from jax.experimental import pallas as pl
from jax.experimental.pallas import tpu as pltpu
from jax.sharding import PartitionSpec as P

HEAD = 128
STEPS = 4
ROWS = 4
HEADS = 8
TOKENS = STEPS * ROWS
QUERIES = STEPS * HEADS
TP = 8
QUAD = 4
PLANE = 32
KB = 5

ADAPTER_SCALE = 2.0
NORM_EPS = 1e-06
MESH = pl.DeviceIdType.MESH
BF = jnp.bfloat16
F32 = jnp.float32


def dot(a, b):
    return jnp.dot(a, b, preferred_element_type=F32)


def dot_t(a, b):
    return lax.dot_general(a, b, (((1,), (1,)), ((), ())), preferred_element_type=F32)


def kernel(
    hidden_hbm, queries_hbm, keys_hbm, values_hbm, lengths_hbm, weight_hbm, down_hbm, up_hbm, gain_hbm,
    o32, e32,
    hidden_v, queries_v, keys_v, values_v, lengths_s, weight_v, down_v, up_v, gain_v,
    hf, rowf, q32, acc32, top32, total32, tiles, hall, detour, bbuf, usend, urecv,
    loc_sem, kv_sem, block_send, block_recv, quad_send, quad_recv, tile_send, tile_recv, b_sem, detour_send, detour_recv, u_send, u_recv,
):
    g = lax.axis_index("group")
    t = lax.axis_index("tp")
    xy, zh, c = g // 4, (g // 2) % 2, g % 2
    z = zh * TP + t
    me = xy * 2 + c
    low, high = zh == 0, zh == 1

    def at_z(where):
        return (xy * 4 + (where // TP) * 2 + c, where % TP)

    def in_plane(i):
        p = jnp.where(i < me, i, i + 1)
        return ((p // 2) * 4 + zh * 2 + p % 2, t)

    def remote(src, dst, send, recv, to):
        return pltpu.make_async_remote_copy(
            src_ref=src, dst_ref=dst, send_sem=send, recv_sem=recv, device_id=to, device_id_type=MESH
        )

    def wait_bytes(ref, sem):
        pltpu.make_async_copy(ref, ref, sem).wait()

    def times(start, stop, body):
        def step(i, _):
            body(i)
            return 0

        lax.fori_loop(start, stop, step, 0)

    small = [
        pltpu.make_async_copy(src, dst, loc_sem.at[i])
        for i, (src, dst) in enumerate(
            (
                (hidden_hbm, hidden_v),
                (down_hbm, down_v),
                (up_hbm, up_v),
                (queries_hbm, queries_v),
                (lengths_hbm, lengths_s),
                (gain_hbm, gain_v),
                (weight_hbm, weight_v),
            )
        )
    ]

    barrier = pltpu.get_barrier_semaphore()

    def greet(to):
        pl.semaphore_signal(barrier, inc=1, device_id=to, device_id_type=MESH)

    def greet_z(d):
        greet(at_z((z - d + 2 * TP) % (2 * TP)))

        @pl.when(z + d < 2 * TP)
        def _():
            greet(at_z(z + d))

    times(1, QUAD + 1, greet_z)

    @pl.when(low)
    def _():
        greet(at_z(z + TP))

    @pl.when(z == 12)
    def _():
        greet(at_z(7))

    @pl.when(z >= TP + 5)
    def _():
        greet(at_z(5))

    times(0, PLANE - 1, lambda i: greet(in_plane(i)))

    for copy in small[:6]:
        copy.start()
    kv = []
    for r in range(ROWS):
        kv.append(
            (
                pltpu.make_async_copy(keys_hbm.at[r], keys_v.at[r], kv_sem.at[0, r]),
                pltpu.make_async_copy(values_hbm.at[r], values_v.at[r], kv_sem.at[1, r]),
            )
        )
        kv[r][0].start()
        kv[r][1].start()
    small[6].start()

    small[0].wait()
    for s in range(STEPS):
        hf[s * ROWS : (s + 1) * ROWS, :] = hidden_v[s].astype(F32)
    for k in range(KB):
        hall[z, k] = hf[:, k * HEAD : (k + 1) * HEAD].astype(BF)
    small[1].wait()
    small[2].wait()
    down = down_v[...].astype(F32)
    up = up_v[...].astype(F32)
    rowf[...] = jnp.zeros_like(rowf)
    for k in range(KB):
        rowf[k : k + 1, :] = down[:, k * HEAD : (k + 1) * HEAD]
    for k in range(2):
        rowf[KB + k : KB + k + 1, :] = up[:, k * HEAD : (k + 1) * HEAD]
    mine = pl.ds(pl.multiple_of(me * 8, 8), 8)
    tiles[0, mine, :] = rowf[0:8, :]
    hall[z, KB] = rowf[...].astype(BF)

    @pl.when(low)
    def _():
        extra = jnp.where(t == 5, 3, jnp.where(t == 7, 1, 0))
        pl.semaphore_wait(barrier, PLANE - 1 + QUAD + jnp.minimum(t, QUAD) + extra)

    @pl.when(high)
    def _():
        pl.semaphore_wait(barrier, PLANE + 2 * QUAD)

    first_quad = t < QUAD
    above, below = (z + QUAD) % (2 * TP), (z + 2 * TP - QUAD) % (2 * TP)
    sends_up = first_quad
    sends_down = jnp.logical_not(first_quad)
    passes = jnp.logical_and(low, sends_down)
    detours = jnp.logical_and(low, jnp.logical_and(t >= 4, t != 5))
    direct = z == 5

    def up_copy():
        return remote(hall.at[z], hall.at[z], block_send.at[0], block_recv.at[0], at_z(above))

    def down_copy():
        block = hall.at[z, pl.ds(0, KB)]
        return remote(block, block, block_send.at[1], block_recv.at[1], at_z(below))

    def pass_copy():
        return remote(hall.at[below], hall.at[below], block_send.at[2], block_recv.at[2], at_z(above))

    def direct_copy():
        return remote(hall.at[z], hall.at[z], block_send.at[0], block_recv.at[2], at_z((z + TP) % (2 * TP)))

    def detour_copy():
        slot = jnp.where(t == 7, 1, 0)
        to = jnp.where(t == 4, 7, 5)
        return remote(hall.at[z], detour.at[slot], detour_send.at[2], detour_recv.at[slot], at_z(to))

    def detour_on(slot, owner):
        return remote(detour.at[slot], hall.at[owner], detour_send.at[slot], block_recv.at[2], at_z(owner + TP))

    def send_on(slot, owner):
        wait_bytes(detour.at[slot], detour_recv.at[slot])
        detour_on(slot, owner).start()

    def from_below():
        wait_bytes(hall.at[below], block_recv.at[0])

    def from_above():
        wait_bytes(hall.at[above, pl.ds(0, KB)], block_recv.at[1])

    apart = jnp.where(first_quad, QUAD, -QUAD)
    corner = z - t % QUAD

    def quad_copy(which, j):
        where = z + which * apart
        block = hall.at[where, pl.ds(0, KB)]
        to = corner + (t + 1 + j) % QUAD
        return remote(block, block, quad_send.at[which, j], quad_recv.at[which, j], at_z(to))

    def quad_arrived(which, j):
        where = corner + (t + 2 * QUAD - 1 - j) % QUAD + which * apart
        wait_bytes(hall.at[where, pl.ds(0, KB)], quad_recv.at[which, j])

    def tile_copy(which, i):
        return remote(
            tiles.at[which, mine], tiles.at[which, mine], tile_send.at[which], tile_recv.at[which], in_plane(i)
        )

    def send_down():
        @pl.when(sends_down)
        def _():
            down_copy().start()

    def b_copy():
        return remote(bbuf.at[0], bbuf.at[1], b_sem.at[0], b_sem.at[1], at_z(z - TP))

    @pl.when(low)
    def _():
        @pl.when(detours)
        def _():
            detour_copy().start()

        @pl.when(direct)
        def _():
            direct_copy().start()

        @pl.when(sends_up)
        def _():
            up_copy().start()

    times(0, PLANE - 1, lambda i: tile_copy(0, i).start())

    @pl.when(jnp.logical_and(low, first_quad))
    def _():
        times(0, QUAD - 1, lambda j: quad_copy(0, j).start())
        from_above()
        times(0, QUAD - 1, lambda j: quad_copy(1, j).start())

    @pl.when(jnp.logical_and(low, jnp.logical_not(first_quad)))
    def _():
        @pl.when(t == 7)
        def _():
            send_on(0, 4)

        from_below()

        @pl.when(passes)
        def _():
            pass_copy().start()

        @pl.when(t == 5)
        def _():
            send_on(0, 6)
            send_on(1, 7)

        send_down()

    @pl.when(high)
    def _():
        send_down()

    @pl.when(jnp.logical_and(high, first_quad))
    def _():
        up_copy().start()

    def rows_of(which, k):
        return tiles[which, pl.ds(k, PLANE, stride=8), :].astype(BF)

    def factor_of(which):
        return jnp.concatenate(
            [jnp.concatenate([rows_of(which, k)] * 4, axis=0) for k in range(KB)], axis=1
        )

    def block_of(where):
        return jnp.concatenate([hall[where, k] for k in range(KB)], axis=1)

    def parts(block, a):
        u = dot_t(block, a)
        first = u.astype(BF).astype(F32)
        rest = u - first
        second = rest.astype(BF).astype(F32)
        third = (rest - second).astype(BF).astype(F32)
        lane = lax.broadcasted_iota(jnp.int32, u.shape, 1)
        zero = jnp.zeros_like(u)
        packed = jnp.where(lane < 32, first, jnp.where(lane < 64, second, jnp.where(lane < 96, third, zero)))
        return packed.astype(BF)

    def u_copy(src, which, where, send, to):
        return remote(src, urecv.at[which, where], u_send.at[send], u_recv.at[which], to)

    small[3].wait()
    for s in range(STEPS):
        for h in range(HEADS):
            q32[pl.ds(s * HEADS + h, ROWS, stride=QUERIES), :] = queries_v[
                s, :, h * HEAD : (h + 1) * HEAD
            ].astype(F32)
    small[4].wait()
    factor = HEAD ** (-0.5)

    def cached(r):
        wait_bytes(keys_v.at[r], kv_sem.at[0, r])
        own = pl.ds(pl.multiple_of(r * QUERIES, QUERIES), QUERIES)
        scores = dot_t(q32[own, :].astype(BF), keys_v[r]) * factor
        slot = lax.broadcasted_iota(jnp.int32, scores.shape, 1)
        scores = jnp.where(slot < lengths_s[r], scores, -jnp.inf)
        top = jnp.max(scores, axis=1, keepdims=True)
        p = jnp.exp(scores - top)
        total = jnp.sum(p, axis=1, keepdims=True)
        wait_bytes(values_v.at[r], kv_sem.at[1, r])
        acc32[own, :] = dot(p.astype(BF), values_v[r])
        top32[own, :] = jnp.broadcast_to(top, (QUERIES, HEAD))
        total32[own, :] = jnp.broadcast_to(total, (QUERIES, HEAD))

    times(0, ROWS, cached)

    wait_bytes(tiles.at[0, pl.ds(0, 8 * PLANE - 8)], tile_recv.at[0])
    a_own = factor_of(0)

    for k in range(2):
        bbuf[0, :, k * HEAD : (k + 1) * HEAD] = rows_of(0, KB + k)

    @pl.when(high)
    def _():
        b_copy().start()
        wait_bytes(hall.at[t], block_recv.at[2])

        def rows_on():
            tiles[1, mine, :] = hall[t, KB].astype(F32)[0:8]
            times(0, PLANE - 1, lambda i: tile_copy(1, i).start())

        pl.when(t >= 6)(rows_on)
        usend[...] = parts(block_of(t), a_own)
        times(0, TP, lambda i: u_copy(usend, 1, t, 1, (g - 2, i)).start())
        pl.when(t < 6)(rows_on)
        times(0, QUAD - 1, lambda j: quad_copy(0, j).start())

    urecv[0, t] = parts(block_of(z), a_own)

    def own_copy(which, send, i):
        return u_copy(urecv.at[which, t], which, t, send, (g, (t + 1 + i) % TP))

    @pl.when(low)
    def _():
        times(0, TP - 1, lambda i: own_copy(0, 0, i).start())

    @pl.when(jnp.logical_and(low, jnp.logical_not(first_quad)))
    def _():
        times(0, QUAD - 1, lambda j: quad_copy(0, j).start())
        times(0, QUAD - 1, lambda j: quad_copy(1, j).start())

    @pl.when(high)
    def _():
        @pl.when(first_quad)
        def _():
            from_above()

        @pl.when(jnp.logical_not(first_quad))
        def _():
            from_below()

        times(0, QUAD - 1, lambda j: quad_copy(1, j).start())
        times(0, TP - 1, lambda i: own_copy(0, 0, i).start())
        wait_bytes(tiles.at[1, pl.ds(0, 8 * PLANE - 8)], tile_recv.at[1])
        urecv[1, t] = parts(block_of(z), factor_of(1))
        times(0, TP - 1, lambda i: own_copy(1, 2, i).start())
        for k in range(2):
            bbuf[1, :, k * HEAD : (k + 1) * HEAD] = rows_of(1, KB + k)

    for which in range(2):
        times(0, QUAD - 1, lambda j, which=which: quad_arrived(which, j))
    small[6].wait()

    def project(i, sofar):
        depth = KB * HEAD
        return sofar + dot(block_of(zh * TP + i), weight_v[pl.ds(pl.multiple_of(i * depth, depth), depth), :])

    base = lax.fori_loop(0, TP, project, jnp.zeros((TOKENS, 2 * HEAD), F32))
    small[5].wait()
    gain = gain_v[...].reshape(1, HEAD)

    def update(which):
        b = jnp.concatenate([bbuf[which]] * 4, axis=0)
        return dot(urecv[which].reshape(TP * TOKENS, HEAD), b)

    def fold(x):
        return ADAPTER_SCALE * jnp.sum(x.reshape(TP, TOKENS, 2 * HEAD), axis=0)

    wait_bytes(urecv.at[0, pl.ds(0, TP - 1)], u_recv.at[0])
    base = base + fold(update(0))

    @pl.when(low)
    def _():
        wait_bytes(bbuf.at[1], b_sem.at[1])
        wait_bytes(urecv.at[1], u_recv.at[1])

    @pl.when(high)
    def _():
        wait_bytes(urecv.at[1, pl.ds(0, TP - 1)], u_recv.at[1])

    projected = base + fold(update(1))

    raw = projected[:, 0:HEAD]
    value = projected[:, HEAD : 2 * HEAD]
    scale = lax.rsqrt(jnp.mean(raw * raw, axis=1, keepdims=True) + NORM_EPS)
    key = raw * scale * gain
    e32[:, 0:HEAD] = key
    e32[:, HEAD : 2 * HEAD] = value

    scores = dot_t(q32[...].astype(BF), key.astype(BF)) * factor
    qi = lax.broadcasted_iota(jnp.int32, scores.shape, 0)
    ki = lax.broadcasted_iota(jnp.int32, scores.shape, 1)
    seen = (ki % ROWS == qi // QUERIES) & (ki // ROWS <= (qi % QUERIES) // HEADS)
    scores = jnp.where(seen, scores, -jnp.inf)
    top_c = top32[:, 0:1]
    top = jnp.maximum(top_c, jnp.max(scores, axis=1, keepdims=True))
    p = jnp.exp(scores - top)
    carry = jnp.exp(top_c - top)
    total = carry * total32[:, 0:1] + jnp.sum(p, axis=1, keepdims=True)
    o32[...] = (carry * acc32[...] + dot(p.astype(BF), value.astype(BF))) / total

    @pl.when(sends_up)
    def _():
        up_copy().wait_send()

    @pl.when(sends_down)
    def _():
        down_copy().wait_send()

    @pl.when(passes)
    def _():
        pass_copy().wait_send()

    @pl.when(detours)
    def _():
        detour_copy().wait_send()

    @pl.when(jnp.logical_or(z == 5, z == 7))
    def _():
        detour_on(0, jnp.where(z == 5, 6, 4)).wait_send()

    @pl.when(z == 5)
    def _():
        detour_on(1, 7).wait_send()

    @pl.when(direct)
    def _():
        direct_copy().wait_send()

    for which in range(2):
        times(0, QUAD - 1, lambda j, which=which: quad_copy(which, j).wait_send())
    wait_bytes(tiles.at[0, pl.ds(0, 8 * PLANE - 8)], tile_send.at[0])
    wait_bytes(urecv.at[0, pl.ds(0, TP - 1)], u_send.at[0])

    @pl.when(high)
    def _():
        wait_bytes(urecv.at[1], u_send.at[1])
        wait_bytes(urecv.at[1, pl.ds(0, TP - 1)], u_send.at[2])
        b_copy().wait_send()
        wait_bytes(tiles.at[1, pl.ds(0, 8 * PLANE - 8)], tile_send.at[1])


def write_out(o32, e32, att_ref, ent_ref):
    for s in range(STEPS):
        ent_ref[s] = e32[s * ROWS : (s + 1) * ROWS, :].astype(BF)
        for h in range(HEADS):
            att_ref[s, :, h * HEAD : (h + 1) * HEAD] = o32[
                pl.ds(s * HEADS + h, ROWS, stride=QUERIES), :
            ].astype(BF)


def per_device(hidden, queries, keys, values, lengths, weight, down, up, gain):
    dma = pltpu.SemaphoreType.DMA
    attention, entries = pl.pallas_call(
        kernel,
        name="decode",
        out_shape=(
            pltpu.VMEM((ROWS * QUERIES, HEAD), F32),
            pltpu.VMEM((TOKENS, 2 * HEAD), F32),
        ),
        in_specs=[pl.BlockSpec(memory_space=pltpu.HBM)] * 9,
        out_specs=(pl.BlockSpec(memory_space=pltpu.VMEM),) * 2,
        scratch_shapes=[
            pltpu.VMEM(hidden.shape, BF),
            pltpu.VMEM(queries.shape, BF),
            pltpu.VMEM(keys.shape, BF),
            pltpu.VMEM(values.shape, BF),
            pltpu.SMEM(lengths.shape, jnp.int32),
            pltpu.VMEM(weight.shape, BF),
            pltpu.VMEM(down.shape, BF),
            pltpu.VMEM(up.shape, BF),
            pltpu.VMEM(gain.shape, F32),
            pltpu.VMEM((TOKENS, KB * HEAD), F32),
            pltpu.VMEM((TOKENS, HEAD), F32),
            pltpu.VMEM((ROWS * QUERIES, HEAD), F32),
            pltpu.VMEM((ROWS * QUERIES, HEAD), F32),
            pltpu.VMEM((ROWS * QUERIES, HEAD), F32),
            pltpu.VMEM((ROWS * QUERIES, HEAD), F32),
            pltpu.VMEM((2, PLANE * 8, HEAD), F32),
            pltpu.VMEM((2 * TP, KB + 1, TOKENS, HEAD), BF),
            pltpu.VMEM((2, KB + 1, TOKENS, HEAD), BF),
            pltpu.VMEM((2, PLANE, 2 * HEAD), BF),
            pltpu.VMEM((TOKENS, HEAD), BF),
            pltpu.VMEM((2, TP, TOKENS, HEAD), BF),
            dma((7,)),
            dma((2, ROWS)),
            dma((3,)),
            dma((3,)),
            dma((2, QUAD - 1)),
            dma((2, QUAD - 1)),
            dma((2,)),
            dma((2,)),
            dma((2,)),
            dma((3,)),
            dma((2,)),
            dma((3,)),
            dma((2,)),
        ],
        compiler_params=pltpu.CompilerParams(
            collective_id=0, has_side_effects=True, vmem_limit_bytes=60 * 1024 * 1024
        ),
    )(hidden, queries, keys, values, lengths, weight, down, up, gain)
    return pl.pallas_call(
        write_out,
        name="write_out",
        out_shape=(
            jax.ShapeDtypeStruct(queries.shape, BF),
            jax.ShapeDtypeStruct((STEPS, ROWS, 2 * HEAD), BF),
        ),
        in_specs=[pl.BlockSpec(memory_space=pltpu.VMEM)] * 2,
        out_specs=(pl.BlockSpec(memory_space=pltpu.VMEM),) * 2,
        compiler_params=pltpu.CompilerParams(vmem_limit_bytes=2 * 1024 * 1024),
    )(attention, entries)


def solution(mesh):
    return jax.shard_map(
        per_device,
        mesh=mesh,
        in_specs=(
            P(None, "group", "tp"),
            P(None, "group", "tp"),
            P("group", None, "tp"),
            P("group", None, "tp"),
            P("group"),
            P(None, "tp"),
            P("group", "tp"),
            P("group", "tp"),
            P(),
        ),
        out_specs=(P(None, "group", "tp"), P(None, "group", "tp")),
        check_vma=False,
    )
```

```python
import jax
import jax.numpy as jnp
from jax import lax
from jax.experimental import pallas as pl
from jax.experimental.pallas import tpu as pltpu
from jax.sharding import PartitionSpec as P

HEAD = 128
STEPS = 4
ROWS = 4
HEADS = 8
TOKENS = STEPS * ROWS
QUERIES = STEPS * HEADS
TP = 8
QUAD = 4
PLANE = 32
KB = 5

ADAPTER_SCALE = 2.0
NORM_EPS = 1e-06
MESH = pl.DeviceIdType.MESH
BF = jnp.bfloat16
F32 = jnp.float32


def dot(a, b):
    return jnp.dot(a, b, preferred_element_type=F32)


def dot_t(a, b):
    return lax.dot_general(a, b, (((1,), (1,)), ((), ())), preferred_element_type=F32)


def kernel(
    hidden_hbm, queries_hbm, keys_hbm, values_hbm, lengths_hbm, weight_hbm, down_hbm, up_hbm, gain_hbm,
    o32, e32,
    hidden_v, queries_v, keys_v, values_v, lengths_s, weight_v, down_v, up_v, gain_v,
    hf, rowf, q32, acc32, top32, total32, tiles, hall, detour, bbuf, usend, urecv,
    loc_sem, kv_sem, block_send, block_recv, quad_send, quad_recv, tile_send, tile_recv, b_sem, detour_send, detour_recv, u_send, u_recv,
):
    g = lax.axis_index("group")
    t = lax.axis_index("tp")
    xy, zh, c = g // 4, (g // 2) % 2, g % 2
    z = zh * TP + t
    me = xy * 2 + c
    low, high = zh == 0, zh == 1

    def at_z(where):
        return (xy * 4 + (where // TP) * 2 + c, where % TP)

    def in_plane(i):
        p = jnp.where(i < me, i, i + 1)
        return ((p // 2) * 4 + zh * 2 + p % 2, t)

    def remote(src, dst, send, recv, to):
        return pltpu.make_async_remote_copy(
            src_ref=src, dst_ref=dst, send_sem=send, recv_sem=recv, device_id=to, device_id_type=MESH
        )

    def wait_bytes(ref, sem):
        pltpu.make_async_copy(ref, ref, sem).wait()

    def times(start, stop, body):
        def step(i, _):
            body(i)
            return 0

        lax.fori_loop(start, stop, step, 0)

    small = [
        pltpu.make_async_copy(src, dst, loc_sem.at[i])
        for i, (src, dst) in enumerate(
            (
                (hidden_hbm, hidden_v),
                (down_hbm, down_v),
                (up_hbm, up_v),
                (queries_hbm, queries_v),
                (lengths_hbm, lengths_s),
                (gain_hbm, gain_v),
                (weight_hbm, weight_v),
            )
        )
    ]

    barrier = pltpu.get_barrier_semaphore()

    def greet(to):
        pl.semaphore_signal(barrier, inc=1, device_id=to, device_id_type=MESH)

    def greet_z(d):
        greet(at_z((z - d + 2 * TP) % (2 * TP)))

        @pl.when(z + d < 2 * TP)
        def _():
            greet(at_z(z + d))

    times(1, QUAD + 1, greet_z)

    @pl.when(low)
    def _():
        greet(at_z(z + TP))

    @pl.when(z == 12)
    def _():
        greet(at_z(7))

    @pl.when(z >= TP + 5)
    def _():
        greet(at_z(5))

    times(0, PLANE - 1, lambda i: greet(in_plane(i)))

    for copy in small[:6]:
        copy.start()
    kv = []
    for r in range(ROWS):
        kv.append(
            (
                pltpu.make_async_copy(keys_hbm.at[r], keys_v.at[r], kv_sem.at[0, r]),
                pltpu.make_async_copy(values_hbm.at[r], values_v.at[r], kv_sem.at[1, r]),
            )
        )
        kv[r][0].start()
        kv[r][1].start()
    small[6].start()

    small[0].wait()
    for s in range(STEPS):
        hf[s * ROWS : (s + 1) * ROWS, :] = hidden_v[s].astype(F32)
    for k in range(KB):
        hall[z, k] = hf[:, k * HEAD : (k + 1) * HEAD].astype(BF)
    small[1].wait()
    small[2].wait()
    down = down_v[...].astype(F32)
    up = up_v[...].astype(F32)
    rowf[...] = jnp.zeros_like(rowf)
    for k in range(KB):
        rowf[k : k + 1, :] = down[:, k * HEAD : (k + 1) * HEAD]
    for k in range(2):
        rowf[KB + k : KB + k + 1, :] = up[:, k * HEAD : (k + 1) * HEAD]
    mine = pl.ds(pl.multiple_of(me * 8, 8), 8)
    tiles[0, mine, :] = rowf[0:8, :]
    hall[z, KB] = rowf[...].astype(BF)

    @pl.when(low)
    def _():
        extra = jnp.where(t == 5, 3, jnp.where(t == 7, 1, 0))
        pl.semaphore_wait(barrier, PLANE - 1 + QUAD + jnp.minimum(t, QUAD) + extra)

    @pl.when(high)
    def _():
        pl.semaphore_wait(barrier, PLANE + 2 * QUAD)

    first_quad = t < QUAD
    above, below = (z + QUAD) % (2 * TP), (z + 2 * TP - QUAD) % (2 * TP)
    sends_up = first_quad
    sends_down = jnp.logical_not(first_quad)
    passes = jnp.logical_and(low, sends_down)
    detours = jnp.logical_and(low, jnp.logical_and(t >= 4, t != 5))
    direct = z == 5

    def up_copy():
        return remote(hall.at[z], hall.at[z], block_send.at[0], block_recv.at[0], at_z(above))

    def down_copy():
        block = hall.at[z, pl.ds(0, KB)]
        return remote(block, block, block_send.at[1], block_recv.at[1], at_z(below))

    def pass_copy():
        return remote(hall.at[below], hall.at[below], block_send.at[2], block_recv.at[2], at_z(above))

    def direct_copy():
        return remote(hall.at[z], hall.at[z], block_send.at[0], block_recv.at[2], at_z((z + TP) % (2 * TP)))

    def detour_copy():
        slot = jnp.where(t == 7, 1, 0)
        to = jnp.where(t == 4, 7, 5)
        return remote(hall.at[z], detour.at[slot], detour_send.at[2], detour_recv.at[slot], at_z(to))

    def detour_on(slot, owner):
        return remote(detour.at[slot], hall.at[owner], detour_send.at[slot], block_recv.at[2], at_z(owner + TP))

    def send_on(slot, owner):
        wait_bytes(detour.at[slot], detour_recv.at[slot])
        detour_on(slot, owner).start()

    def from_below():
        wait_bytes(hall.at[below], block_recv.at[0])

    def from_above():
        wait_bytes(hall.at[above, pl.ds(0, KB)], block_recv.at[1])

    apart = jnp.where(first_quad, QUAD, -QUAD)
    corner = z - t % QUAD

    def quad_copy(which, j):
        where = z + which * apart
        block = hall.at[where, pl.ds(0, KB)]
        to = corner + (t + 1 + j) % QUAD
        return remote(block, block, quad_send.at[which, j], quad_recv.at[which, j], at_z(to))

    def quad_arrived(which, j):
        where = corner + (t + 2 * QUAD - 1 - j) % QUAD + which * apart
        wait_bytes(hall.at[where, pl.ds(0, KB)], quad_recv.at[which, j])

    def tile_copy(which, i):
        return remote(
            tiles.at[which, mine], tiles.at[which, mine], tile_send.at[which], tile_recv.at[which], in_plane(i)
        )

    def send_down():
        @pl.when(sends_down)
        def _():
            down_copy().start()

    def b_copy():
        return remote(bbuf.at[0], bbuf.at[1], b_sem.at[0], b_sem.at[1], at_z(z - TP))

    @pl.when(low)
    def _():
        @pl.when(detours)
        def _():
            detour_copy().start()

        @pl.when(direct)
        def _():
            direct_copy().start()

        @pl.when(sends_up)
        def _():
            up_copy().start()

    times(0, PLANE - 1, lambda i: tile_copy(0, i).start())

    @pl.when(jnp.logical_and(low, first_quad))
    def _():
        times(0, QUAD - 1, lambda j: quad_copy(0, j).start())

    @pl.when(jnp.logical_and(low, jnp.logical_not(first_quad)))
    def _():
        @pl.when(t == 7)
        def _():
            send_on(0, 4)

        from_below()

        @pl.when(passes)
        def _():
            pass_copy().start()

        @pl.when(t == 5)
        def _():
            send_on(0, 6)
            send_on(1, 7)

        send_down()

    @pl.when(high)
    def _():
        send_down()

    @pl.when(jnp.logical_and(high, first_quad))
    def _():
        up_copy().start()

    def rows_of(which, k):
        return tiles[which, pl.ds(k, PLANE, stride=8), :].astype(BF)

    def factor_of(which):
        return jnp.concatenate(
            [jnp.concatenate([rows_of(which, k)] * 4, axis=0) for k in range(KB)], axis=1
        )

    def block_of(where):
        return jnp.concatenate([hall[where, k] for k in range(KB)], axis=1)

    def parts(block, a):
        u = dot_t(block, a)
        first = u.astype(BF).astype(F32)
        rest = u - first
        second = rest.astype(BF).astype(F32)
        third = (rest - second).astype(BF).astype(F32)
        lane = lax.broadcasted_iota(jnp.int32, u.shape, 1)
        zero = jnp.zeros_like(u)
        packed = jnp.where(lane < 32, first, jnp.where(lane < 64, second, jnp.where(lane < 96, third, zero)))
        return packed.astype(BF)

    def u_copy(src, which, where, send, to):
        return remote(src, urecv.at[which, where], u_send.at[send], u_recv.at[which], to)

    small[3].wait()
    for s in range(STEPS):
        for h in range(HEADS):
            q32[pl.ds(s * HEADS + h, ROWS, stride=QUERIES), :] = queries_v[
                s, :, h * HEAD : (h + 1) * HEAD
            ].astype(F32)
    small[4].wait()
    factor = HEAD ** (-0.5)

    def cached(r):
        wait_bytes(keys_v.at[r], kv_sem.at[0, r])
        own = pl.ds(pl.multiple_of(r * QUERIES, QUERIES), QUERIES)
        scores = dot_t(q32[own, :].astype(BF), keys_v[r]) * factor
        slot = lax.broadcasted_iota(jnp.int32, scores.shape, 1)
        scores = jnp.where(slot < lengths_s[r], scores, -jnp.inf)
        top = jnp.max(scores, axis=1, keepdims=True)
        p = jnp.exp(scores - top)
        total = jnp.sum(p, axis=1, keepdims=True)
        wait_bytes(values_v.at[r], kv_sem.at[1, r])
        acc32[own, :] = dot(p.astype(BF), values_v[r])
        top32[own, :] = jnp.broadcast_to(top, (QUERIES, HEAD))
        total32[own, :] = jnp.broadcast_to(total, (QUERIES, HEAD))

    times(0, ROWS, cached)

    @pl.when(jnp.logical_and(low, first_quad))
    def _():
        from_above()
        times(0, QUAD - 1, lambda j: quad_copy(1, j).start())

    wait_bytes(tiles.at[0, pl.ds(0, 8 * PLANE - 8)], tile_recv.at[0])
    a_own = factor_of(0)

    for k in range(2):
        bbuf[0, :, k * HEAD : (k + 1) * HEAD] = rows_of(0, KB + k)

    @pl.when(high)
    def _():
        b_copy().start()
        wait_bytes(hall.at[t], block_recv.at[2])

        def rows_on():
            tiles[1, mine, :] = hall[t, KB].astype(F32)[0:8]
            times(0, PLANE - 1, lambda i: tile_copy(1, i).start())

        pl.when(t >= 6)(rows_on)
        usend[...] = parts(block_of(t), a_own)
        times(0, TP, lambda i: u_copy(usend, 1, t, 1, (g - 2, i)).start())
        pl.when(t < 6)(rows_on)
        times(0, QUAD - 1, lambda j: quad_copy(0, j).start())

    urecv[0, t] = parts(block_of(z), a_own)

    def own_copy(which, send, i):
        return u_copy(urecv.at[which, t], which, t, send, (g, jnp.where(i < t, i, i + 1)))

    @pl.when(low)
    def _():
        times(0, TP - 1, lambda i: own_copy(0, 0, i).start())

    @pl.when(jnp.logical_and(low, jnp.logical_not(first_quad)))
    def _():
        times(0, QUAD - 1, lambda j: quad_copy(0, j).start())
        times(0, QUAD - 1, lambda j: quad_copy(1, j).start())

    @pl.when(high)
    def _():
        @pl.when(first_quad)
        def _():
            from_above()

        @pl.when(jnp.logical_not(first_quad))
        def _():
            from_below()

        times(0, QUAD - 1, lambda j: quad_copy(1, j).start())
        times(0, TP - 1, lambda i: own_copy(0, 0, i).start())
        wait_bytes(tiles.at[1, pl.ds(0, 8 * PLANE - 8)], tile_recv.at[1])
        urecv[1, t] = parts(block_of(z), factor_of(1))
        times(0, TP - 1, lambda i: own_copy(1, 2, i).start())
        for k in range(2):
            bbuf[1, :, k * HEAD : (k + 1) * HEAD] = rows_of(1, KB + k)

    for which in range(2):
        times(0, QUAD - 1, lambda j, which=which: quad_arrived(which, j))
    small[6].wait()

    def project(i, sofar):
        depth = KB * HEAD
        return sofar + dot(block_of(zh * TP + i), weight_v[pl.ds(pl.multiple_of(i * depth, depth), depth), :])

    base = lax.fori_loop(0, TP, project, jnp.zeros((TOKENS, 2 * HEAD), F32))
    small[5].wait()
    gain = gain_v[...].reshape(1, HEAD)

    def update(which):
        b = jnp.concatenate([bbuf[which]] * 4, axis=0)
        return dot(urecv[which].reshape(TP * TOKENS, HEAD), b)

    def fold(x):
        return ADAPTER_SCALE * jnp.sum(x.reshape(TP, TOKENS, 2 * HEAD), axis=0)

    wait_bytes(urecv.at[0, pl.ds(0, TP - 1)], u_recv.at[0])
    base = base + fold(update(0))

    @pl.when(low)
    def _():
        wait_bytes(bbuf.at[1], b_sem.at[1])
        wait_bytes(urecv.at[1], u_recv.at[1])

    @pl.when(high)
    def _():
        wait_bytes(urecv.at[1, pl.ds(0, TP - 1)], u_recv.at[1])

    projected = base + fold(update(1))

    raw = projected[:, 0:HEAD]
    value = projected[:, HEAD : 2 * HEAD]
    scale = lax.rsqrt(jnp.mean(raw * raw, axis=1, keepdims=True) + NORM_EPS)
    key = raw * scale * gain
    e32[:, 0:HEAD] = key
    e32[:, HEAD : 2 * HEAD] = value

    scores = dot_t(q32[...].astype(BF), key.astype(BF)) * factor
    qi = lax.broadcasted_iota(jnp.int32, scores.shape, 0)
    ki = lax.broadcasted_iota(jnp.int32, scores.shape, 1)
    seen = (ki % ROWS == qi // QUERIES) & (ki // ROWS <= (qi % QUERIES) // HEADS)
    scores = jnp.where(seen, scores, -jnp.inf)
    top_c = top32[:, 0:1]
    top = jnp.maximum(top_c, jnp.max(scores, axis=1, keepdims=True))
    p = jnp.exp(scores - top)
    carry = jnp.exp(top_c - top)
    total = carry * total32[:, 0:1] + jnp.sum(p, axis=1, keepdims=True)
    o32[...] = (carry * acc32[...] + dot(p.astype(BF), value.astype(BF))) / total

    @pl.when(sends_up)
    def _():
        up_copy().wait_send()

    @pl.when(sends_down)
    def _():
        down_copy().wait_send()

    @pl.when(passes)
    def _():
        pass_copy().wait_send()

    @pl.when(detours)
    def _():
        detour_copy().wait_send()

    @pl.when(jnp.logical_or(z == 5, z == 7))
    def _():
        detour_on(0, jnp.where(z == 5, 6, 4)).wait_send()

    @pl.when(z == 5)
    def _():
        detour_on(1, 7).wait_send()

    @pl.when(direct)
    def _():
        direct_copy().wait_send()

    for which in range(2):
        times(0, QUAD - 1, lambda j, which=which: quad_copy(which, j).wait_send())
    wait_bytes(tiles.at[0, pl.ds(0, 8 * PLANE - 8)], tile_send.at[0])
    wait_bytes(urecv.at[0, pl.ds(0, TP - 1)], u_send.at[0])

    @pl.when(high)
    def _():
        wait_bytes(urecv.at[1], u_send.at[1])
        wait_bytes(urecv.at[1, pl.ds(0, TP - 1)], u_send.at[2])
        b_copy().wait_send()
        wait_bytes(tiles.at[1, pl.ds(0, 8 * PLANE - 8)], tile_send.at[1])


def write_out(o32, e32, att_ref, ent_ref):
    for s in range(STEPS):
        ent_ref[s] = e32[s * ROWS : (s + 1) * ROWS, :].astype(BF)
        for h in range(HEADS):
            att_ref[s, :, h * HEAD : (h + 1) * HEAD] = o32[
                pl.ds(s * HEADS + h, ROWS, stride=QUERIES), :
            ].astype(BF)


def per_device(hidden, queries, keys, values, lengths, weight, down, up, gain):
    dma = pltpu.SemaphoreType.DMA
    attention, entries = pl.pallas_call(
        kernel,
        name="decode",
        out_shape=(
            pltpu.VMEM((ROWS * QUERIES, HEAD), F32),
            pltpu.VMEM((TOKENS, 2 * HEAD), F32),
        ),
        in_specs=[pl.BlockSpec(memory_space=pltpu.HBM)] * 9,
        out_specs=(pl.BlockSpec(memory_space=pltpu.VMEM),) * 2,
        scratch_shapes=[
            pltpu.VMEM(hidden.shape, BF),
            pltpu.VMEM(queries.shape, BF),
            pltpu.VMEM(keys.shape, BF),
            pltpu.VMEM(values.shape, BF),
            pltpu.SMEM(lengths.shape, jnp.int32),
            pltpu.VMEM(weight.shape, BF),
            pltpu.VMEM(down.shape, BF),
            pltpu.VMEM(up.shape, BF),
            pltpu.VMEM(gain.shape, F32),
            pltpu.VMEM((TOKENS, KB * HEAD), F32),
            pltpu.VMEM((TOKENS, HEAD), F32),
            pltpu.VMEM((ROWS * QUERIES, HEAD), F32),
            pltpu.VMEM((ROWS * QUERIES, HEAD), F32),
            pltpu.VMEM((ROWS * QUERIES, HEAD), F32),
            pltpu.VMEM((ROWS * QUERIES, HEAD), F32),
            pltpu.VMEM((2, PLANE * 8, HEAD), F32),
            pltpu.VMEM((2 * TP, KB + 1, TOKENS, HEAD), BF),
            pltpu.VMEM((2, KB + 1, TOKENS, HEAD), BF),
            pltpu.VMEM((2, PLANE, 2 * HEAD), BF),
            pltpu.VMEM((TOKENS, HEAD), BF),
            pltpu.VMEM((2, TP, TOKENS, HEAD), BF),
            dma((7,)),
            dma((2, ROWS)),
            dma((3,)),
            dma((3,)),
            dma((2, QUAD - 1)),
            dma((2, QUAD - 1)),
            dma((2,)),
            dma((2,)),
            dma((2,)),
            dma((3,)),
            dma((2,)),
            dma((3,)),
            dma((2,)),
        ],
        compiler_params=pltpu.CompilerParams(
            collective_id=0, has_side_effects=True, vmem_limit_bytes=60 * 1024 * 1024
        ),
    )(hidden, queries, keys, values, lengths, weight, down, up, gain)
    return pl.pallas_call(
        write_out,
        name="write_out",
        out_shape=(
            jax.ShapeDtypeStruct(queries.shape, BF),
            jax.ShapeDtypeStruct((STEPS, ROWS, 2 * HEAD), BF),
        ),
        in_specs=[pl.BlockSpec(memory_space=pltpu.VMEM)] * 2,
        out_specs=(pl.BlockSpec(memory_space=pltpu.VMEM),) * 2,
        compiler_params=pltpu.CompilerParams(vmem_limit_bytes=2 * 1024 * 1024),
    )(attention, entries)


def solution(mesh):
    return jax.shard_map(
        per_device,
        mesh=mesh,
        in_specs=(
            P(None, "group", "tp"),
            P(None, "group", "tp"),
            P("group", None, "tp"),
            P("group", None, "tp"),
            P("group"),
            P(None, "tp"),
            P("group", "tp"),
            P("group", "tp"),
            P(),
        ),
        out_specs=(P(None, "group", "tp"), P(None, "group", "tp")),
        check_vma=False,
    )
```
